256 devices in a mesh: band: 64 (over y, z, core), pos: 4 (over x).
Axes of the slice: x: 4, y: 4, z: 8, core: 2. Of those that a mesh axis runs over, the one named last changes fastest.
Arguments:
- object_field: float32 [2, 12288, 512], P(None, 'band'), may hold values from -6 to 6
- probe: float32 [2, 256, 256], replicated, may hold values from -6 to 6
- measured: bfloat16 [3072, 256, 256], P(('band', 'pos')), may hold values from 0 to 2
- row_offset: int32 [3072], P(('band', 'pos')), may hold values from 0 to 191
- col_offset: int32 [3072], P(('band', 'pos')), may hold values from 0 to 256
- counts: int32 [256], P(('band', 'pos')), may hold values from 1 to 12, 1024 in all
Outputs:
- object_grad: float32 [2, 12288, 512], P(None, 'band')
- probe_grad: float32 [2, 256, 256], replicated
The draws below stay inside these ranges and needn't reach their ends.
Inputs may be any that keep to these rules, and one draw needn't show every extreme that they name: The counts sum to 1024; the busiest device has exactly 12 live slots.
All inputs are finite; a program needn't handle non-finite values.
Results may differ from the reference program's by a relative error of at most 0.0018.
The reference program's roundings to bfloat16 on the way count: a program that leaves them out, or rounds other values in their place, can miss the bound.
Values may be sent and summed in bfloat16 or wider, within the bound.
A program may use at most 64 MiB of HBM per device.

```python
import math
import jax
import jax.numpy as jnp
import numpy as np
from jax import lax

W = 256
BR = 192
NCOLS = 512
CAP = 12
SHARDS = 256
SLOTS = 3072
LIVE = 1024
NROWS = 12288
N_POS = 4


def with_ends(result, stream_key, smallest, largest):
    longest = result.shape.index(max(result.shape))
    spots = []
    for shift in (0, 1):
        where = [jax.random.randint(jax.random.fold_in(stream_key, axis), (), 0, length) for axis, length in enumerate(result.shape)]
        where[longest] = (where[longest] + shift) % result.shape[longest]
        spots.append(tuple(where))
    return result.at[spots[0]].set(smallest).at[spots[1]].set(largest)


def block_scale(rng, shape, split, smallest, largest):
    factor_of, own = 1.0, jax.random.fold_in(rng, 6)
    for axis_at, shards_of in split:
        heights = jnp.exp(jax.random.uniform(jax.random.fold_in(own, axis_at), (shards_of,), jnp.float32, smallest / len(split), largest / len(split)))
        factor_of = factor_of * jnp.repeat(heights, shape[axis_at] // shards_of).reshape([-1 if axis == axis_at else 1 for axis in range(len(shape))])
    return factor_of


def profile(count, total, most, skew):
    weights = [(1 << 20) // math.isqrt(rank ** skew) + 1 for rank in range(2, count + 1)]
    spare, given = total - most - (count - 1), [1] * (count - 1)
    while spare > 0:
        movable = [i for i in range(count - 1) if given[i] < most]
        mass, left = sum([weights[i] for i in movable]), spare
        for i in movable:
            extra = min(most - given[i], max(1, left * weights[i] // mass), spare)
            given[i] = given[i] + extra
            spare = spare - extra
    return np.array([most] + given)


def uneven_parts(rng, count, total, reach, lean):
    if count == 2:
        one = jax.random.randint(rng, (), max(1, total - reach), min(reach, total - 1) + 1)
        return jnp.stack([one, total - one])
    lengths = jnp.asarray(profile(count, total, reach, lean), jnp.int32)
    pairs = (count - 1) // 2
    giver, receiver = lengths[1:1 + 2 * pairs:2], lengths[2:2 + 2 * pairs:2]
    slack = jnp.minimum(giver - 1, reach - receiver)
    shifted = jax.random.randint(jax.random.fold_in(rng, 1), (pairs,), 0, 1 << 20) % (slack + 1)
    lengths = lengths.at[1:1 + 2 * pairs:2].set(giver - shifted).at[2:2 + 2 * pairs:2].set(receiver + shifted)
    return lengths[jax.random.permutation(jax.random.fold_in(rng, 2), count)]


def normal_values(stream_key, shape, spread, bound, split=(), kind=jnp.bfloat16):
    values = jax.random.normal(stream_key, shape, jnp.float32) * spread
    if len(split) > 0:
        values = block_scale(stream_key, shape, split, -0.22, 0.18) * values
    return jnp.clip(values, min=-bound, max=bound).astype(kind)


def setup_inputs(seed: int = 0) -> dict:
    key_of = jax.random.split(jax.random.key(seed), 7)
    return {
        "object_field": normal_values(key_of[0], (2, NROWS, NCOLS), 0.7, 6.0, ((1, 64),), jnp.float32),
        "probe": normal_values(key_of[1], (2, W, W), 0.7, 6.0, (), jnp.float32),
        "measured": jnp.clip(2.0 * jax.random.uniform(key_of[2], (SLOTS, W, W), jnp.float32) ** block_scale(key_of[2], (SLOTS, W, W), ((0, 256),), -0.2, 0.2), 0.0, 2.0).astype(jnp.bfloat16),
        "row_offset": with_ends(jax.random.randint(key_of[3], (SLOTS,), 0, BR), jax.random.fold_in(key_of[3], 1), 0, BR - 1).astype(jnp.int32),
        "col_offset": with_ends(jax.random.randint(key_of[4], (SLOTS,), 0, NCOLS - W + 1), jax.random.fold_in(key_of[4], 1), 0, NCOLS - W).astype(jnp.int32),
        "counts": uneven_parts(key_of[5], SHARDS, LIVE, CAP, 2).astype(jnp.int32),
    }


def dft_tables(width):
    index = jnp.arange(width, dtype=jnp.int32)
    phase = index[:, None] * index[None, :] % width
    angle = phase.astype(jnp.float32) * (2.0 * math.pi / width)
    factor = 1.0 / math.sqrt(width)
    real_part = (jnp.cos(angle) * factor).astype(jnp.bfloat16)
    imag_part = (-jnp.sin(angle) * factor).astype(jnp.bfloat16)
    left_table = jnp.concatenate([jnp.concatenate([real_part, -imag_part], 1), jnp.concatenate([imag_part, real_part], 1)], 0)
    right_table = jnp.concatenate([jnp.concatenate([real_part, imag_part], 1), jnp.concatenate([-imag_part, real_part], 1)], 0)
    return (left_table, right_table)

def slot_terms(patch, probe, measured_one, live, left_table, right_table):
    width = probe.shape[1]
    patch_f = patch.astype(jnp.float32)
    exit_real = probe[0] * patch_f[0] - probe[1] * patch_f[1]
    exit_imag = probe[0] * patch_f[1] + probe[1] * patch_f[0]
    exit_wave = jnp.concatenate([exit_real, exit_imag], 0).astype(jnp.bfloat16)
    half = jnp.dot(left_table, exit_wave, preferred_element_type=jnp.float32).astype(jnp.bfloat16)
    half_row = jnp.concatenate([half[:width], half[width:]], 1)
    wave = jnp.dot(half_row, right_table, preferred_element_type=jnp.float32)
    wave_real = wave[:, :width]
    wave_imag = wave[:, width:]
    excess = (wave_real * wave_real + wave_imag * wave_imag - measured_one.astype(jnp.float32)) * live
    resid = jnp.concatenate([wave_real * excess, wave_imag * excess], 1).astype(jnp.bfloat16)
    back = jnp.dot(resid, left_table, preferred_element_type=jnp.float32).astype(jnp.bfloat16)
    back_col = jnp.concatenate([back[:, :width], back[:, width:]], 0)
    chi = jnp.dot(right_table, back_col, preferred_element_type=jnp.float32)
    chi_real = chi[:width]
    chi_imag = chi[width:]
    grad_patch = jnp.stack([probe[0] * chi_real + probe[1] * chi_imag, probe[0] * chi_imag - probe[1] * chi_real])
    probe_term = jnp.stack([patch_f[0] * chi_real + patch_f[1] * chi_imag, patch_f[0] * chi_imag - patch_f[1] * chi_real])
    return (grad_patch, probe_term)

def reference(object_field, probe, measured, row_offset, col_offset, counts):
    width = probe.shape[1]
    columns = object_field.shape[2]
    lowered = object_field.astype(jnp.bfloat16)
    padded = jnp.concatenate([lowered, jnp.zeros((2, width, columns), jnp.bfloat16)], 1)
    left_table, right_table = dft_tables(width)

    def visit(carry, index):
        shard = index // CAP
        band = shard // N_POS
        top = (band * BR + row_offset[index]).astype(jnp.int32)
        start = col_offset[index].astype(jnp.int32)
        zero = jnp.int32(0)

        def work(state):
            grad, probe_sum = state
            patch = lax.dynamic_slice(padded, (zero, top, start), (2, width, width))
            grad_patch, probe_term = slot_terms(patch, probe, measured[index], 1.0, left_table, right_table)
            current = lax.dynamic_slice(grad, (zero, top, start), (2, width, width))
            grad = lax.dynamic_update_slice(grad, current + grad_patch, (zero, top, start))
            return (grad, probe_sum + probe_term)

        def skip(state):
            return state
        live = index % CAP < counts[shard]
        return (lax.cond(live, work, skip, carry), None)
    initial = (jnp.zeros((2, NROWS + width, columns), jnp.float32), jnp.zeros((2, width, width), jnp.float32))
    (grad, probe_sum), _ = lax.scan(visit, initial, jnp.arange(SLOTS, dtype=jnp.int32))
    return (grad[:, :NROWS], probe_sum * (1.0 / math.sqrt(LIVE)))
```

```python
import math

import jax
import jax.numpy as jnp
import ml_dtypes
import numpy as np
from jax import lax
from jax.experimental import pallas as pl
from jax.experimental.pallas import tpu as pltpu
from jax.sharding import PartitionSpec as P

W = 256
BR = 192
NCOLS = 512
CAP = 12
LIVE = 1024
LANES = 128
BLOCKS = NCOLS // LANES
TAIL = 64
ROWS = 2 * BR + TAIL
CHIP = ROWS + BR
HALF = CHIP // 2
NX, NY, NZ = 4, 4, 8
CHIPS = NY * NZ
BANDS = 2 * CHIPS
F32 = jnp.float32
BF16 = jnp.bfloat16
MESH = pl.DeviceIdType.MESH


def tables():
    index = np.arange(W, dtype=np.int32)
    phase = index[:, None] * index[None, :] % W
    angle = phase.astype(np.float32) * np.float32(2.0 * math.pi / W)
    factor = np.float32(1.0 / math.sqrt(W))
    real = (np.cos(angle) * factor).astype(ml_dtypes.bfloat16)
    imag = (-np.sin(angle) * factor).astype(ml_dtypes.bfloat16)
    left = np.block([[real, -imag], [imag, real]])
    right = np.block([[real, imag], [-imag, real]])
    return left, right


def dot(a, b):
    return jnp.dot(a, b, preferred_element_type=F32)


def remote(src, dst, send, recv, device):
    return pltpu.make_async_remote_copy(
        src_ref=src, dst_ref=dst, send_sem=send, recv_sem=recv, device_id=device, device_id_type=MESH
    )


def signal(barrier, device):
    pl.semaphore_signal(barrier, inc=1, device_id=device, device_id_type=MESH)


def halo_kernel(obj, win, low, near, far, send, recv):
    b = lax.axis_index("band")
    barrier = pltpu.get_barrier_semaphore()
    for step in (1, 2):

        @pl.when(b + step < BANDS)
        def _():
            signal(barrier, {"band": b + step})

    low[...] = obj[...].astype(BF16)

    def copies(step):
        src, dst = (low, near) if step == 1 else (low.at[:, :TAIL], far)
        return [
            remote(src.at[plane], dst.at[plane], send.at[step - 1, plane], recv.at[step - 1, plane], {"band": b - step})
            for plane in range(2)
        ]


    @pl.when(b > 0)
    def _():
        pl.semaphore_wait(barrier, jnp.minimum(b, 2))

    for step in (1, 2):

        @pl.when(b >= step)
        def _():
            for copy in copies(step):
                copy.start()

    def fill(src, top, count):
        for plane in range(2):
            for block in range(BLOCKS):
                win[plane, block, top : top + count] = src[plane, :, block * LANES : (block + 1) * LANES].astype(F32)

    fill(low, 0, BR)
    for step, src, top, count in ((1, near, BR, BR), (2, far, 2 * BR, TAIL)):

        @pl.when(b + step < BANDS)
        def _():
            for copy in copies(step):
                copy.wait_recv()
            fill(src, top, count)

        @pl.when(b + step >= BANDS)
        def _():
            win[:, :, top : top + count] = jnp.zeros((2, BLOCKS, count, LANES), F32)

    for step in (1, 2):

        @pl.when(b >= step)
        def _():
            for copy in copies(step):
                copy.wait_send()


def slots_kernel(cnt, row, col, win, probe, meas, left, right, grad, psum, mbuf, sems):
    n = cnt[0]

    def fetch(s):
        return pltpu.make_async_copy(meas.at[s], mbuf.at[s], sems.at[s])

    def start(s, carry):
        fetch(s).start()
        return carry

    lax.fori_loop(0, n, start, 0)
    grad[...] = jnp.zeros_like(grad)
    psum[...] = jnp.zeros_like(psum)
    lane = lax.broadcasted_iota(jnp.int32, (W, LANES), 1)

    def body(s, carry):
        r = row[s]
        c = col[s]
        block = jnp.where(c >= LANES, 1, 0)
        shift = c - LANES * block
        back = lax.rem(LANES - shift, LANES)
        ahead = lax.rem(shift, LANES)
        head = lane < LANES - shift

        def patch(plane):
            parts = [pltpu.roll(win[plane, block + j, pl.ds(r, W), :], back, 1) for j in range(3)]
            return jnp.concatenate([jnp.where(head, parts[0], parts[1]), jnp.where(head, parts[1], parts[2])], 1)

        pr, pi = patch(0), patch(1)
        qr, qi = probe[0], probe[1]
        exit_wave = jnp.concatenate([qr * pr - qi * pi, qr * pi + qi * pr], 0).astype(BF16)
        half = dot(left[...], exit_wave).astype(BF16)
        wave = dot(jnp.concatenate([half[:W], half[W:]], 1), right[...])
        wr, wi = wave[:, :W], wave[:, W:]
        fetch(s).wait()
        excess = wr * wr + wi * wi - mbuf[s].astype(F32)
        resid = jnp.concatenate([wr * excess, wi * excess], 1).astype(BF16)
        back_wave = dot(resid, left[...]).astype(BF16)
        chi = dot(right[...], jnp.concatenate([back_wave[:, :W], back_wave[:, W:]], 0))
        cr, ci = chi[:W], chi[W:]
        psum[0] += pr * cr + pi * ci
        psum[1] += pr * ci - pi * cr
        tail = lane >= shift
        for plane, g in enumerate((qr * cr + qi * ci, qr * ci - qi * cr)):
            g0 = pltpu.roll(g[:, :LANES], ahead, 1)
            g1 = pltpu.roll(g[:, LANES:], ahead, 1)
            grad[plane, block, pl.ds(r, W), :] += jnp.where(tail, g0, 0.0)
            grad[plane, block + 1, pl.ds(r, W), :] += jnp.where(tail, g1, g0)
            grad[plane, block + 2, pl.ds(r, W), :] += jnp.where(tail, 0.0, g1)
        return carry

    lax.fori_loop(0, n, body, 0)


def merge_kernel(
    grad, psum, out, pout,
    from_core, merged, relay_l, relay_r, from_l, from_r, from_z, final,
    pcore, psumc, py, pz, px,
    core_s, core_r, ring_s, ring_r, shift_s, shift_r, out_s, out_r, loc, pc_s, pc_r, y_s, y_r, z_s, z_r, x_s, x_r,
):
    b = lax.axis_index("band")
    p = lax.axis_index("pos")
    core = lax.rem(b, 2)
    chip = b // 2
    z = lax.rem(chip, NZ)
    y = chip // NZ
    sib = {"band": b + 1 - 2 * core}
    rp = lax.rem(p + 1, NX)
    lp = lax.rem(p + NX - 1, NX)
    op = lax.rem(p + 2, NX)
    left, right = {"pos": lp}, {"pos": rp}
    ydev = [None] + [{"band": b + 2 * NZ * (lax.rem(y + d, NY) - y)} for d in range(1, NY)]
    zdev = [None] + [{"band": b + 2 * (lax.rem(z + d, NZ) - z)} for d in range(1, NZ)]
    xdev = [None] + [{"pos": lax.rem(p + d, NX)} for d in range(1, NX)]
    sb = b + 1 - 2 * core

    barrier = pltpu.get_barrier_semaphore()
    for device in [sib, {"band": sb, "pos": lp}, {"band": sb, "pos": rp}] + xdev[1:] + ydev[1:] + zdev[1:]:
        signal(barrier, device)

    @pl.when(chip > 0)
    def _():
        signal(barrier, {"band": b - 2})

    @pl.when(chip < CHIPS - 1)
    def _():
        signal(barrier, {"band": b + 2})

    edges = jnp.where(chip > 0, 1, 0) + jnp.where(chip < CHIPS - 1, 1, 0)
    pl.semaphore_wait(barrier, 3 + NX - 1 + NY - 1 + NZ - 1 + edges)

    order = [op, rp, lp, p]
    to_core = [
        remote(grad.at[j // 2, 2 * (1 - core) + lax.rem(j, 2)], from_core.at[j], core_s.at[i], core_r.at[i], sib)
        for i, j in enumerate(order)
    ]
    pcopy = remote(psum.at[1 - core], pcore, pc_s.at[0], pc_r.at[0], sib)
    for copy in to_core:
        copy.start()
    pcopy.start()

    def merge(i):
        j = order[i]
        to_core[i].wait_recv()
        merged[j, pl.ds(ROWS * (1 - core), BR), :] = jnp.zeros((BR, LANES), F32)
        merged[j, pl.ds(BR * core, ROWS), :] = grad[j // 2, 2 * core + lax.rem(j, 2)]
        merged[j, pl.ds(BR * (1 - core), ROWS), :] += from_core[j]

    top, low = pl.ds(0, HALF), pl.ds(HALF, HALF)
    a_r = remote(merged.at[op, top], relay_l, ring_s.at[0], ring_r.at[0], right)
    a_l = remote(merged.at[op, low], relay_r, ring_s.at[1], ring_r.at[1], left)
    b_r = remote(merged.at[rp, low], from_l.at[low], ring_s.at[2], ring_r.at[2], right)
    b_l = remote(merged.at[lp, top], from_r.at[top], ring_s.at[3], ring_r.at[3], left)
    c_r = remote(merged.at[rp, top], from_l.at[top], ring_s.at[4], ring_r.at[4], right)
    c_l = remote(merged.at[lp, low], from_r.at[low], ring_s.at[5], ring_r.at[5], left)
    merge(0)
    a_r.start()
    a_l.start()
    merge(1)
    b_r.start()
    merge(2)
    b_l.start()

    pcopy.wait_recv()
    psumc[...] = psum[core] + pcore[...]
    yc = [None]
    for d in range(1, NY):
        yd = lax.rem(y + d, NY)
        yc.append(remote(psumc.at[pl.ds(64 * yd, 64)], py.at[d], y_s.at[d], y_r.at[d], ydev[d]))
        yc[d].start()

    a_r.wait_recv()
    merged[rp, top, :] += relay_l[...]
    c_r.start()
    a_l.wait_recv()
    merged[lp, low, :] += relay_r[...]
    c_l.start()
    merge(3)

    for d in range(1, NY):
        yc[d].wait_recv()
    py[0] = psumc[pl.ds(64 * y, 64), :] + py[1] + py[2] + py[3]
    zc = [None]
    for d in range(1, NZ):
        zd = lax.rem(z + d, NZ)
        zc.append(remote(py.at[0, pl.ds(8 * zd, 8)], pz.at[d], z_s.at[d], z_r.at[d], zdev[d]))
        zc[d].start()

    b_r.wait_recv()
    b_l.wait_recv()

    for d in range(1, NZ):
        zc[d].wait_recv()
    px[p] = ((py[0, pl.ds(8 * z, 8), :] + pz[1]) + (pz[2] + pz[3])) + ((pz[4] + pz[5]) + (pz[6] + pz[7]))
    xc = [None]
    for d in range(1, NX):
        xc.append(remote(px.at[p], px.at[p], x_s.at[d], x_r.at[d], xdev[d]))
        xc[d].start()

    c_l.wait_recv()
    c_r.wait_recv()
    own, below = pl.ds(0, 2 * BR), pl.ds(2 * BR, CHIP - 2 * BR)
    final[below, :] = merged[p, below, :] + (from_l[below, :] + from_r[below, :])
    shift = remote(final.at[below], from_z, shift_s.at[0], shift_r.at[0], {"band": b + 2})

    @pl.when(chip < CHIPS - 1)
    def _():
        shift.start()

    final[own, :] = merged[p, own, :] + (from_l[own, :] + from_r[own, :])

    for d in range(1, NX):
        xc[d].wait_recv()
    zrows = pl.ds(8 * z, 8)
    prow = pl.ds(64 * y + 8 * z, 8)
    total = ((px[0] + px[1]) + (px[2] + px[3])) * F32(1.0 / math.sqrt(LIVE))
    pout[core, prow, :] = total
    zg = [None]
    for d in range(1, NZ):
        zg.append(remote(pout.at[core, prow], pout.at[core, prow], z_s.at[NZ + d], z_r.at[NZ + d], zdev[d]))
        zg[d].start()

    @pl.when(chip > 0)
    def _():
        shift.wait_recv()
        final[pl.ds(0, CHIP - 2 * BR), :] += from_z[...]

    plane = p // 2
    cols = pl.ds(pl.multiple_of(LANES * (2 * core + lax.rem(p, 2)), LANES), LANES)
    gather = []
    for c in range(2):
        src = final.at[pl.ds(BR * c, BR)]
        dst = out.at[plane, :, cols]
        for i, pos in enumerate((rp, lp)):
            k = 2 * i + c
            gather.append(remote(src, dst, out_s.at[k], out_r.at[2 * i + core], {"band": 2 * chip + c, "pos": pos}))
    for copy in gather:
        copy.start()
    sibcopy = remote(final.at[pl.ds(BR * (1 - core), BR)], out.at[plane, :, cols], out_s.at[4], out_r.at[4], sib)
    sibcopy.start()
    mine = pltpu.make_async_copy(final.at[pl.ds(BR * core, BR)], out.at[plane, :, cols], loc)
    mine.start()

    for d in range(1, NZ):
        zg[d].wait_recv()
    yrows = pl.ds(64 * y, 64)
    yg = [None]
    for d in range(1, NY):
        yg.append(remote(pout.at[core, yrows], pout.at[core, yrows], y_s.at[NY + d], y_r.at[NY + d], ydev[d]))
        yg[d].start()

    def got(i, c, pos):
        blk = pl.ds(pl.multiple_of(LANES * (2 * c + lax.rem(pos, 2)), LANES), LANES)
        return out.at[pos // 2, :, blk], out_r.at[2 * i + c]

    ref_l0, sem_l0 = got(0, 0, lp)
    ref_l1, sem_l1 = got(0, 1, lp)
    ref_r0, sem_r0 = got(1, 0, rp)
    ref_r1, sem_r1 = got(1, 1, rp)
    on_r = remote(ref_l0, ref_l0, out_s.at[5], out_r.at[5], right)
    on_l = remote(ref_r1, ref_r1, out_s.at[6], out_r.at[6], left)
    remote(ref_l0, ref_l0, out_s.at[0], sem_l0, right).wait_recv()
    on_r.start()
    remote(ref_r1, ref_r1, out_s.at[0], sem_r1, right).wait_recv()
    on_l.start()

    for d in range(1, NY):
        yg[d].wait_recv()
    plast = remote(pout.at[core], pout.at[core], pc_s.at[1], pc_r.at[1], sib)
    plast.start()

    remote(ref_l1, ref_l1, out_s.at[0], sem_l1, right).wait_recv()
    remote(ref_r0, ref_r0, out_s.at[0], sem_r0, right).wait_recv()
    sibcopy.wait_recv()
    on_r.wait_recv()
    on_l.wait_recv()
    plast.wait_recv()
    mine.wait()

    for copy in to_core + [pcopy, a_r, a_l, b_r, b_l, c_r, c_l] + yc[1:] + zc[1:] + xc[1:] + zg[1:] + yg[1:]:
        copy.wait_send()
    for copy in gather + [sibcopy, on_r, on_l, plast]:
        copy.wait_send()

    @pl.when(chip < CHIPS - 1)
    def _():
        shift.wait_send()


VM = pl.BlockSpec(memory_space=pltpu.VMEM)
SM = pl.BlockSpec(memory_space=pltpu.SMEM)
ANY = pl.BlockSpec(memory_space=pl.ANY)
DMA = pltpu.SemaphoreType.DMA


def params(cid=None):
    return pltpu.CompilerParams(vmem_limit_bytes=40 << 20, collective_id=cid, has_side_effects=cid is not None)


def halo(obj):
    return pl.pallas_call(
        halo_kernel,
        out_shape=jax.ShapeDtypeStruct((2, BLOCKS, ROWS, LANES), F32),
        in_specs=[VM],
        out_specs=VM,
        scratch_shapes=[
            pltpu.VMEM((2, BR, NCOLS), BF16),
            pltpu.VMEM((2, BR, NCOLS), BF16),
            pltpu.VMEM((2, TAIL, NCOLS), BF16),
            DMA((2, 2)),
            DMA((2, 2)),
        ],
        compiler_params=params(0),
        name="halo",
    )(obj)


def slots(counts, rows, cols, win, probe, measured, left, right):
    return pl.pallas_call(
        slots_kernel,
        out_shape=(
            jax.ShapeDtypeStruct((2, BLOCKS, ROWS, LANES), F32),
            jax.ShapeDtypeStruct((2, W, W), F32),
        ),
        in_specs=[SM, SM, SM, VM, VM, ANY, VM, VM],
        out_specs=(VM, VM),
        scratch_shapes=[pltpu.VMEM((CAP, W, W), BF16), DMA((CAP,))],
        compiler_params=params(),
        name="slots",
    )(counts, rows, cols, win, probe, measured, left, right)


def merge(grad, psum):
    piece = lambda n, *lead: pltpu.VMEM((*lead, n, LANES), F32)
    flat = lambda n, *lead: pltpu.VMEM((*lead, n, W), F32)
    return pl.pallas_call(
        merge_kernel,
        out_shape=(
            jax.ShapeDtypeStruct((2, BR, NCOLS), F32),
            jax.ShapeDtypeStruct((2, W, W), F32),
        ),
        in_specs=[VM, VM],
        out_specs=(VM, VM),
        scratch_shapes=[
            piece(ROWS, 4),
            piece(CHIP, 4),
            piece(HALF),
            piece(HALF),
            piece(CHIP),
            piece(CHIP),
            piece(CHIP - 2 * BR),
            piece(CHIP),
            flat(W),
            flat(W),
            flat(64, NY),
            flat(8, NZ),
            flat(8, NX),
            DMA((4,)), DMA((4,)),
            DMA((6,)), DMA((6,)),
            DMA((1,)), DMA((1,)),
            DMA((7,)), DMA((7,)),
            DMA,
            DMA((2,)), DMA((2,)),
            DMA((2 * NY,)), DMA((2 * NY,)),
            DMA((2 * NZ,)), DMA((2 * NZ,)),
            DMA((NX,)), DMA((NX,)),
        ],
        compiler_params=params(1),
        name="merge",
    )(grad, psum)


def on_device(object_field, probe, measured, row_offset, col_offset, counts):
    left, right = tables()
    win = halo(object_field)
    grad, psum = slots(counts, row_offset, col_offset, win, probe, measured, left, right)
    return merge(grad, psum)


def solution(mesh):
    placed = (
        P(None, "band", None),
        P(),
        P(("band", "pos"), None, None),
        P(("band", "pos")),
        P(("band", "pos")),
        P(("band", "pos")),
    )
    return jax.shard_map(
        on_device,
        mesh=mesh,
        in_specs=placed,
        out_specs=(P(None, "band", None), P()),
        check_vma=False,
    )
```

```python
import math

import jax
import jax.numpy as jnp
import ml_dtypes
import numpy as np
from jax import lax
from jax.experimental import pallas as pl
from jax.experimental.pallas import tpu as pltpu
from jax.sharding import PartitionSpec as P

W = 256
BR = 192
NCOLS = 512
CAP = 12
GROUP = 6
LIVE = 1024
LANES = 128
BLOCKS = NCOLS // LANES
TAIL = 64
ROWS = 2 * BR + TAIL
CHIP = ROWS + BR
HALF = CHIP // 2
NX, NY, NZ = 4, 4, 8
CHIPS = NY * NZ
BANDS = 2 * CHIPS
F32 = jnp.float32
BF16 = jnp.bfloat16
MESH = pl.DeviceIdType.MESH


def tables():
    index = np.arange(W, dtype=np.int32)
    phase = index[:, None] * index[None, :] % W
    angle = phase.astype(np.float32) * np.float32(2.0 * math.pi / W)
    factor = np.float32(1.0 / math.sqrt(W))
    real = (np.cos(angle) * factor).astype(ml_dtypes.bfloat16)
    imag = (-np.sin(angle) * factor).astype(ml_dtypes.bfloat16)
    left = np.block([[real, -imag], [imag, real]])
    right = np.block([[real, imag], [-imag, real]])
    return left, right


def dot(a, b):
    return jnp.dot(a, b, preferred_element_type=F32)


def remote(src, dst, send, recv, device):
    return pltpu.make_async_remote_copy(
        src_ref=src, dst_ref=dst, send_sem=send, recv_sem=recv, device_id=device, device_id_type=MESH
    )


def signal(barrier, device):
    pl.semaphore_signal(barrier, inc=1, device_id=device, device_id_type=MESH)


def halo_kernel(obj, win, low, near, far, send, recv):
    b = lax.axis_index("band")
    barrier = pltpu.get_barrier_semaphore()
    for step in (1, 2):

        @pl.when(b + step < BANDS)
        def _():
            signal(barrier, {"band": b + step})

    low[...] = obj[...].astype(BF16)

    def copies(step):
        src, dst = (low, near) if step == 1 else (low.at[:, :TAIL], far)
        return [
            remote(src.at[plane], dst.at[plane], send.at[step - 1, plane], recv.at[step - 1, plane], {"band": b - step})
            for plane in range(2)
        ]


    @pl.when(b > 0)
    def _():
        pl.semaphore_wait(barrier, jnp.minimum(b, 2))

    for step in (1, 2):

        @pl.when(b >= step)
        def _():
            for copy in copies(step):
                copy.start()

    def fill(src, top, count):
        for plane in range(2):
            for block in range(BLOCKS):
                win[plane, block, top : top + count] = src[plane, :, block * LANES : (block + 1) * LANES].astype(F32)

    fill(low, 0, BR)
    for step, src, top, count in ((1, near, BR, BR), (2, far, 2 * BR, TAIL)):

        @pl.when(b + step < BANDS)
        def _():
            for copy in copies(step):
                copy.wait_recv()
            fill(src, top, count)

        @pl.when(b + step >= BANDS)
        def _():
            win[:, :, top : top + count] = jnp.zeros((2, BLOCKS, count, LANES), F32)

    for step in (1, 2):

        @pl.when(b >= step)
        def _():
            for copy in copies(step):
                copy.wait_send()


def slots_kernel(cnt, row, col, win, probe, meas, left, right, grad, psum, mbuf, sems):
    n = cnt[0]

    def fetch(s):
        return pltpu.make_async_copy(meas.at[s], mbuf.at[s], sems.at[s])

    def start(s, carry):
        fetch(s).start()
        return carry

    def finish(s, carry):
        fetch(s).wait()
        return carry

    lax.fori_loop(0, CAP, start, 0)
    grad[...] = jnp.zeros_like(grad)
    psum[...] = jnp.zeros_like(psum)
    lane = lax.broadcasted_iota(jnp.int32, (W, LANES), 1)

    def group(i, carry):
        base = GROUP * i
        place, patches, half, resid, spread, chi = ({} for _ in range(6))

        def enter(k):
            s = base + k
            c = col[s]
            block = jnp.where(c >= LANES, 1, 0)
            place[k] = (row[s], block, c - LANES * block)
            r, block, shift = place[k]
            back = lax.rem(LANES - shift, LANES)
            head = lane < LANES - shift
            patch = []
            for plane in range(2):
                parts = [pltpu.roll(win[plane, block + j, pl.ds(r, W), :], back, 1) for j in range(3)]
                patch.append(
                    jnp.concatenate([jnp.where(head, parts[0], parts[1]), jnp.where(head, parts[1], parts[2])], 1)
                )
            patches[k] = patch
            pr, pi = patch
            qr, qi = probe[0], probe[1]
            exit_wave = jnp.concatenate([qr * pr - qi * pi, qr * pi + qi * pr], 0).astype(BF16)
            half[k] = dot(left[...], exit_wave).astype(BF16)

        def detect(k):
            wave = dot(jnp.concatenate([half[k][:W], half[k][W:]], 1), right[...])
            wr, wi = wave[:, :W], wave[:, W:]
            live = jnp.where(base + k < n, F32(1.0), F32(0.0))
            excess = (wr * wr + wi * wi - mbuf[base + k].astype(F32)) * live
            resid[k] = jnp.concatenate([wr * excess, wi * excess], 1).astype(BF16)

        def over_columns(k):
            spread[k] = dot(resid[k], left[...]).astype(BF16)

        def over_rows(k):
            chi[k] = dot(right[...], jnp.concatenate([spread[k][:, :W], spread[k][:, W:]], 0))

        def leave(k):
            r, block, shift = place[k]
            ahead = lax.rem(shift, LANES)
            tail = lane >= shift
            pr, pi = patches[k]
            qr, qi = probe[0], probe[1]
            cr, ci = chi[k][:W], chi[k][W:]
            psum[0] += pr * cr + pi * ci
            psum[1] += pr * ci - pi * cr
            for plane, g in enumerate((qr * cr + qi * ci, qr * ci - qi * cr)):
                g0 = pltpu.roll(g[:, :LANES], ahead, 1)
                g1 = pltpu.roll(g[:, LANES:], ahead, 1)
                grad[plane, block, pl.ds(r, W), :] += jnp.where(tail, g0, 0.0)
                grad[plane, block + 1, pl.ds(r, W), :] += jnp.where(tail, g1, g0)
                grad[plane, block + 2, pl.ds(r, W), :] += jnp.where(tail, 0.0, g1)

        stages = (enter, detect, over_columns, over_rows, leave)
        for t in range(GROUP + len(stages) - 1):
            for at in reversed(range(len(stages))):
                if 0 <= t - at < GROUP:
                    stages[at](t - at)
        return carry

    lax.fori_loop(0, CAP, finish, 0)
    lax.fori_loop(0, (n + GROUP - 1) // GROUP, group, 0)


def merge_kernel(
    grad, psum, out, pout,
    from_core, merged, relay_l, relay_r, from_l, from_r, from_z, final,
    pcore, psumc, py, pz, px,
    core_s, core_r, ring_s, ring_r, shift_s, shift_r, out_s, out_r, loc, pc_s, pc_r, y_s, y_r, z_s, z_r, x_s, x_r,
):
    b = lax.axis_index("band")
    p = lax.axis_index("pos")
    core = lax.rem(b, 2)
    chip = b // 2
    z = lax.rem(chip, NZ)
    y = chip // NZ
    sib = {"band": b + 1 - 2 * core}
    rp = lax.rem(p + 1, NX)
    lp = lax.rem(p + NX - 1, NX)
    op = lax.rem(p + 2, NX)
    left, right = {"pos": lp}, {"pos": rp}
    ydev = [None] + [{"band": b + 2 * NZ * (lax.rem(y + d, NY) - y)} for d in range(1, NY)]
    zdev = [None] + [{"band": b + 2 * (lax.rem(z + d, NZ) - z)} for d in range(1, NZ)]
    xdev = [None] + [{"pos": lax.rem(p + d, NX)} for d in range(1, NX)]
    sb = b + 1 - 2 * core

    barrier = pltpu.get_barrier_semaphore()
    for device in [sib, {"band": sb, "pos": lp}, {"band": sb, "pos": rp}] + xdev[1:] + ydev[1:] + zdev[1:]:
        signal(barrier, device)

    @pl.when(chip > 0)
    def _():
        signal(barrier, {"band": b - 2})

    @pl.when(chip < CHIPS - 1)
    def _():
        signal(barrier, {"band": b + 2})

    edges = jnp.where(chip > 0, 1, 0) + jnp.where(chip < CHIPS - 1, 1, 0)
    pl.semaphore_wait(barrier, 3 + NX - 1 + NY - 1 + NZ - 1 + edges)

    order = [op, rp, lp, p]
    to_core = [
        remote(grad.at[j // 2, 2 * (1 - core) + lax.rem(j, 2)], from_core.at[j], core_s.at[i], core_r.at[i], sib)
        for i, j in enumerate(order)
    ]
    pcopy = remote(psum.at[1 - core], pcore, pc_s.at[0], pc_r.at[0], sib)
    for copy in to_core:
        copy.start()
    pcopy.start()

    def merge(i):
        j = order[i]
        to_core[i].wait_recv()
        merged[j, pl.ds(ROWS * (1 - core), BR), :] = jnp.zeros((BR, LANES), F32)
        merged[j, pl.ds(BR * core, ROWS), :] = grad[j // 2, 2 * core + lax.rem(j, 2)]
        merged[j, pl.ds(BR * (1 - core), ROWS), :] += from_core[j]

    top, low = pl.ds(0, HALF), pl.ds(HALF, HALF)
    a_r = remote(merged.at[op, top], relay_l, ring_s.at[0], ring_r.at[0], right)
    a_l = remote(merged.at[op, low], relay_r, ring_s.at[1], ring_r.at[1], left)
    b_r = remote(merged.at[rp, low], from_l.at[low], ring_s.at[2], ring_r.at[2], right)
    b_l = remote(merged.at[lp, top], from_r.at[top], ring_s.at[3], ring_r.at[3], left)
    c_r = remote(merged.at[rp, top], from_l.at[top], ring_s.at[4], ring_r.at[4], right)
    c_l = remote(merged.at[lp, low], from_r.at[low], ring_s.at[5], ring_r.at[5], left)
    merge(0)
    a_r.start()
    a_l.start()
    merge(1)
    b_r.start()
    merge(2)
    b_l.start()

    pcopy.wait_recv()
    psumc[...] = psum[core] + pcore[...]
    yc = [None]
    for d in range(1, NY):
        yd = lax.rem(y + d, NY)
        yc.append(remote(psumc.at[pl.ds(64 * yd, 64)], py.at[d], y_s.at[d], y_r.at[d], ydev[d]))
        yc[d].start()

    a_r.wait_recv()
    merged[rp, top, :] += relay_l[...]
    c_r.start()
    a_l.wait_recv()
    merged[lp, low, :] += relay_r[...]
    c_l.start()
    merge(3)

    for d in range(1, NY):
        yc[d].wait_recv()
    py[0] = psumc[pl.ds(64 * y, 64), :] + py[1] + py[2] + py[3]
    zc = [None]
    for d in range(1, NZ):
        zd = lax.rem(z + d, NZ)
        zc.append(remote(py.at[0, pl.ds(8 * zd, 8)], pz.at[d], z_s.at[d], z_r.at[d], zdev[d]))
        zc[d].start()

    b_r.wait_recv()
    b_l.wait_recv()

    for d in range(1, NZ):
        zc[d].wait_recv()
    px[p] = ((py[0, pl.ds(8 * z, 8), :] + pz[1]) + (pz[2] + pz[3])) + ((pz[4] + pz[5]) + (pz[6] + pz[7]))
    xc = [None]
    for d in range(1, NX):
        xc.append(remote(px.at[p], px.at[p], x_s.at[d], x_r.at[d], xdev[d]))
        xc[d].start()

    c_l.wait_recv()
    c_r.wait_recv()
    own, below = pl.ds(0, 2 * BR), pl.ds(2 * BR, CHIP - 2 * BR)
    final[below, :] = merged[p, below, :] + (from_l[below, :] + from_r[below, :])
    shift = remote(final.at[below], from_z, shift_s.at[0], shift_r.at[0], {"band": b + 2})

    @pl.when(chip < CHIPS - 1)
    def _():
        shift.start()

    final[own, :] = merged[p, own, :] + (from_l[own, :] + from_r[own, :])

    for d in range(1, NX):
        xc[d].wait_recv()
    zrows = pl.ds(8 * z, 8)
    prow = pl.ds(64 * y + 8 * z, 8)
    total = ((px[0] + px[1]) + (px[2] + px[3])) * F32(1.0 / math.sqrt(LIVE))
    pout[core, prow, :] = total
    zg = [None]
    for d in range(1, NZ):
        zg.append(remote(pout.at[core, prow], pout.at[core, prow], z_s.at[NZ + d], z_r.at[NZ + d], zdev[d]))
        zg[d].start()

    @pl.when(chip > 0)
    def _():
        shift.wait_recv()
        final[pl.ds(0, CHIP - 2 * BR), :] += from_z[...]

    plane = p // 2
    cols = pl.ds(pl.multiple_of(LANES * (2 * core + lax.rem(p, 2)), LANES), LANES)
    gather = []
    for c in range(2):
        src = final.at[pl.ds(BR * c, BR)]
        dst = out.at[plane, :, cols]
        for i, pos in enumerate((rp, lp)):
            k = 2 * i + c
            gather.append(remote(src, dst, out_s.at[k], out_r.at[2 * i + core], {"band": 2 * chip + c, "pos": pos}))
    for copy in gather:
        copy.start()
    sibcopy = remote(final.at[pl.ds(BR * (1 - core), BR)], out.at[plane, :, cols], out_s.at[4], out_r.at[4], sib)
    sibcopy.start()
    mine = pltpu.make_async_copy(final.at[pl.ds(BR * core, BR)], out.at[plane, :, cols], loc)
    mine.start()

    for d in range(1, NZ):
        zg[d].wait_recv()
    yrows = pl.ds(64 * y, 64)
    yg = [None]
    for d in range(1, NY):
        yg.append(remote(pout.at[core, yrows], pout.at[core, yrows], y_s.at[NY + d], y_r.at[NY + d], ydev[d]))
        yg[d].start()

    def got(i, c, pos):
        blk = pl.ds(pl.multiple_of(LANES * (2 * c + lax.rem(pos, 2)), LANES), LANES)
        return out.at[pos // 2, :, blk], out_r.at[2 * i + c]

    ref_l0, sem_l0 = got(0, 0, lp)
    ref_l1, sem_l1 = got(0, 1, lp)
    ref_r0, sem_r0 = got(1, 0, rp)
    ref_r1, sem_r1 = got(1, 1, rp)
    on_r = remote(ref_l0, ref_l0, out_s.at[5], out_r.at[5], right)
    on_l = remote(ref_r1, ref_r1, out_s.at[6], out_r.at[6], left)
    remote(ref_l0, ref_l0, out_s.at[0], sem_l0, right).wait_recv()
    on_r.start()
    remote(ref_r1, ref_r1, out_s.at[0], sem_r1, right).wait_recv()
    on_l.start()

    for d in range(1, NY):
        yg[d].wait_recv()
    plast = remote(pout.at[core], pout.at[core], pc_s.at[1], pc_r.at[1], sib)
    plast.start()

    remote(ref_l1, ref_l1, out_s.at[0], sem_l1, right).wait_recv()
    remote(ref_r0, ref_r0, out_s.at[0], sem_r0, right).wait_recv()
    sibcopy.wait_recv()
    on_r.wait_recv()
    on_l.wait_recv()
    plast.wait_recv()
    mine.wait()

    for copy in to_core + [pcopy, a_r, a_l, b_r, b_l, c_r, c_l] + yc[1:] + zc[1:] + xc[1:] + zg[1:] + yg[1:]:
        copy.wait_send()
    for copy in gather + [sibcopy, on_r, on_l, plast]:
        copy.wait_send()

    @pl.when(chip < CHIPS - 1)
    def _():
        shift.wait_send()


VM = pl.BlockSpec(memory_space=pltpu.VMEM)
SM = pl.BlockSpec(memory_space=pltpu.SMEM)
ANY = pl.BlockSpec(memory_space=pl.ANY)
DMA = pltpu.SemaphoreType.DMA


def params(cid=None):
    return pltpu.CompilerParams(vmem_limit_bytes=40 << 20, collective_id=cid, has_side_effects=cid is not None)


def halo(obj):
    return pl.pallas_call(
        halo_kernel,
        out_shape=jax.ShapeDtypeStruct((2, BLOCKS, ROWS, LANES), F32),
        in_specs=[VM],
        out_specs=VM,
        scratch_shapes=[
            pltpu.VMEM((2, BR, NCOLS), BF16),
            pltpu.VMEM((2, BR, NCOLS), BF16),
            pltpu.VMEM((2, TAIL, NCOLS), BF16),
            DMA((2, 2)),
            DMA((2, 2)),
        ],
        compiler_params=params(0),
        name="halo",
    )(obj)


def slots(counts, rows, cols, win, probe, measured, left, right):
    return pl.pallas_call(
        slots_kernel,
        out_shape=(
            jax.ShapeDtypeStruct((2, BLOCKS, ROWS, LANES), F32),
            jax.ShapeDtypeStruct((2, W, W), F32),
        ),
        in_specs=[SM, SM, SM, VM, VM, ANY, VM, VM],
        out_specs=(VM, VM),
        scratch_shapes=[pltpu.VMEM((CAP, W, W), BF16), DMA((CAP,))],
        compiler_params=params(),
        name="slots",
    )(counts, rows, cols, win, probe, measured, left, right)


def merge(grad, psum):
    piece = lambda n, *lead: pltpu.VMEM((*lead, n, LANES), F32)
    flat = lambda n, *lead: pltpu.VMEM((*lead, n, W), F32)
    return pl.pallas_call(
        merge_kernel,
        out_shape=(
            jax.ShapeDtypeStruct((2, BR, NCOLS), F32),
            jax.ShapeDtypeStruct((2, W, W), F32),
        ),
        in_specs=[VM, VM],
        out_specs=(VM, VM),
        scratch_shapes=[
            piece(ROWS, 4),
            piece(CHIP, 4),
            piece(HALF),
            piece(HALF),
            piece(CHIP),
            piece(CHIP),
            piece(CHIP - 2 * BR),
            piece(CHIP),
            flat(W),
            flat(W),
            flat(64, NY),
            flat(8, NZ),
            flat(8, NX),
            DMA((4,)), DMA((4,)),
            DMA((6,)), DMA((6,)),
            DMA((1,)), DMA((1,)),
            DMA((7,)), DMA((7,)),
            DMA,
            DMA((2,)), DMA((2,)),
            DMA((2 * NY,)), DMA((2 * NY,)),
            DMA((2 * NZ,)), DMA((2 * NZ,)),
            DMA((NX,)), DMA((NX,)),
        ],
        compiler_params=params(1),
        name="merge",
    )(grad, psum)


def on_device(object_field, probe, measured, row_offset, col_offset, counts):
    left, right = tables()
    win = halo(object_field)
    grad, psum = slots(counts, row_offset, col_offset, win, probe, measured, left, right)
    return merge(grad, psum)


def solution(mesh):
    placed = (
        P(None, "band", None),
        P(),
        P(("band", "pos"), None, None),
        P(("band", "pos")),
        P(("band", "pos")),
        P(("band", "pos")),
    )
    return jax.shard_map(
        on_device,
        mesh=mesh,
        in_specs=placed,
        out_specs=(P(None, "band", None), P()),
        check_vma=False,
    )
```

```python
import math

import jax
import jax.numpy as jnp
import ml_dtypes
import numpy as np
from jax import lax
from jax.experimental import pallas as pl
from jax.experimental.pallas import tpu as pltpu
from jax.sharding import PartitionSpec as P

W = 256
BR = 192
NCOLS = 512
CAP = 12
GROUP = 6
LIVE = 1024
LANES = 128
BLOCKS = NCOLS // LANES
TAIL = 64
ROWS = 2 * BR + TAIL
OWN = 2 * BR
BELOW = BR + TAIL
CHIP = OWN + BELOW
EXTRA = 16
TINY = 1e-33
FULL = 16000.0
NX, NY, NZ = 4, 4, 8
CHIPS = NY * NZ
BANDS = 2 * CHIPS
F32 = jnp.float32
BF16 = jnp.bfloat16
MESH = pl.DeviceIdType.MESH


def table():
    index = np.arange(W, dtype=np.int32)
    phase = index[:, None] * index[None, :] % W
    angle = phase.astype(np.float32) * np.float32(2.0 * math.pi / W)
    factor = np.float32(1.0 / math.sqrt(W))
    real = (np.cos(angle) * factor).astype(ml_dtypes.bfloat16)
    imag = (-np.sin(angle) * factor).astype(ml_dtypes.bfloat16)
    return np.concatenate([real, imag], 1).astype(np.float32)


def dot(a, b):
    return jnp.dot(a, b, preferred_element_type=F32)


def remote(src, dst, send, recv, device):
    return pltpu.make_async_remote_copy(
        src_ref=src, dst_ref=dst, send_sem=send, recv_sem=recv, device_id=device, device_id_type=MESH
    )


def signal(barrier, device):
    pl.semaphore_signal(barrier, inc=1, device_id=device, device_id_type=MESH)


def halo_kernel(
    obj, table, probe_in, meas_in, row_in, col_in,
    win, left, right, probe, meas, row, col,
    own, waves, low, near, far, send, recv, load,
):
    b = lax.axis_index("band")
    barrier = pltpu.get_barrier_semaphore()
    for step in (1, 2):

        @pl.when(b + step < BANDS)
        def _():
            signal(barrier, {"band": b + step})

    loads = [pltpu.make_async_copy(obj.at[plane], own.at[plane], load.at[plane]) for plane in range(2)]
    rest = ((table, waves), (row_in, row), (col_in, col), (probe_in, probe), (meas_in, meas))
    loads += [pltpu.make_async_copy(src, dst, load.at[2 + i]) for i, (src, dst) in enumerate(rest)]
    for copy in loads:
        copy.start()
    for plane in range(2):
        loads[plane].wait()
        low[plane] = own[plane].astype(BF16)

    def copies(step):
        src, dst = (low, near) if step == 1 else (low.at[:, :TAIL], far)
        return [
            remote(src.at[plane], dst.at[plane], send.at[step - 1, plane], recv.at[step - 1, plane], {"band": b - step})
            for plane in range(2)
        ]

    @pl.when(b > 0)
    def _():
        pl.semaphore_wait(barrier, jnp.minimum(b, 2))

    for step in (1, 2):

        @pl.when(b >= step)
        def _():
            for copy in copies(step):
                copy.start()

    loads[2].wait()
    real, imag = waves[:, :W], waves[:, W:]
    for rows, first, second in ((0, real, imag), (W, -imag, real)):
        right[rows : rows + W, :W] = first.astype(BF16)
        right[rows : rows + W, W:] = second.astype(BF16)
    for rows, first, second in ((0, real, -imag), (W, imag, real)):
        left[rows : rows + W, :W] = first.astype(BF16)
        left[rows : rows + W, W:] = second.astype(BF16)

    def fill(src, top, count):
        for plane in range(2):
            for block in range(BLOCKS):
                win[plane, block, top : top + count] = src[plane, :, block * LANES : (block + 1) * LANES].astype(F32)

    fill(low, 0, BR)
    for step, src, top, count in ((1, near, BR, BR), (2, far, 2 * BR, TAIL)):

        @pl.when(b + step < BANDS)
        def _():
            for copy in copies(step):
                copy.wait_recv()
            fill(src, top, count)

        @pl.when(b + step >= BANDS)
        def _():
            win[:, :, top : top + count] = jnp.zeros((2, BLOCKS, count, LANES), F32)

    for copy in loads[3:]:
        copy.wait()
    for step in (1, 2):

        @pl.when(b >= step)
        def _():
            for copy in copies(step):
                copy.wait_send()


def slots_kernel(cnt, row, col, win, probe, meas, left, right, grad, psum):
    grad[...] = jnp.zeros_like(grad)
    psum[...] = jnp.zeros_like(psum)
    n = cnt[0]
    lane = lax.broadcasted_iota(jnp.int32, (W, LANES), 1)

    def group(i, carry):
        base = GROUP * i
        place, patches, half, resid, spread, chi = ({} for _ in range(6))

        def enter(k):
            s = base + k
            c = col[s]
            block = jnp.where(c >= LANES, 1, 0)
            place[k] = (row[s], block, c - LANES * block)
            r, block, shift = place[k]
            back = lax.rem(LANES - shift, LANES)
            head = lane < LANES - shift
            patch = []
            for plane in range(2):
                parts = [pltpu.roll(win[plane, block + j, pl.ds(r, W), :], back, 1) for j in range(3)]
                patch.append(
                    jnp.concatenate([jnp.where(head, parts[0], parts[1]), jnp.where(head, parts[1], parts[2])], 1)
                )
            patches[k] = patch
            pr, pi = patch
            qr, qi = probe[0], probe[1]
            exit_wave = jnp.concatenate([qr * pr - qi * pi, qr * pi + qi * pr], 0).astype(BF16)
            half[k] = dot(left[...], exit_wave).astype(BF16)

        def detect(k):
            wave = dot(jnp.concatenate([half[k][:W], half[k][W:]], 1), right[...])
            wr, wi = wave[:, :W], wave[:, W:]
            live = jnp.where(base + k < n, F32(1.0), F32(0.0))
            excess = (wr * wr + wi * wi - meas[base + k].astype(F32)) * live
            resid[k] = jnp.concatenate([wr * excess, wi * excess], 1).astype(BF16)

        def over_columns(k):
            spread[k] = dot(resid[k], left[...]).astype(BF16)

        def over_rows(k):
            chi[k] = dot(right[...], jnp.concatenate([spread[k][:, :W], spread[k][:, W:]], 0))

        def leave(k):
            r, block, shift = place[k]
            ahead = lax.rem(shift, LANES)
            tail = lane >= shift
            pr, pi = patches[k]
            qr, qi = probe[0], probe[1]
            cr, ci = chi[k][:W], chi[k][W:]
            psum[0] += pr * cr + pi * ci
            psum[1] += pr * ci - pi * cr
            for plane, g in enumerate((qr * cr + qi * ci, qr * ci - qi * cr)):
                g0 = pltpu.roll(g[:, :LANES], ahead, 1)
                g1 = pltpu.roll(g[:, LANES:], ahead, 1)
                grad[plane, block, pl.ds(r, W), :] += jnp.where(tail, g0, 0.0)
                grad[plane, block + 1, pl.ds(r, W), :] += jnp.where(tail, g1, g0)
                grad[plane, block + 2, pl.ds(r, W), :] += jnp.where(tail, 0.0, g1)

        stages = (enter, detect, over_columns, over_rows, leave)
        for t in range(GROUP + len(stages) - 1):
            for at in reversed(range(len(stages))):
                if 0 <= t - at < GROUP:
                    stages[at](t - at)
        return carry

    lax.fori_loop(0, (n + GROUP - 1) // GROUP, group, 0)


def signed_power(value):
    most = jnp.maximum(jnp.max(jnp.abs(value), axis=0, keepdims=True), F32(TINY))
    return jnp.floor(jnp.log2(most))


def code(value, dst, rows):
    power = signed_power(value)
    scaled = value * (jnp.exp2(-power) * F32(FULL))
    dst[:rows] = jnp.round(scaled).astype(jnp.int32).astype(jnp.int16)
    dst[rows:] = jnp.broadcast_to(power, (EXTRA, LANES)).astype(jnp.int32).astype(jnp.int16)


def decode(src, rows):
    power = src[rows:].astype(jnp.int32).astype(F32)[:1]
    return src[:rows].astype(jnp.int32).astype(F32) * (jnp.exp2(power) * F32(1.0 / FULL))


def merge_kernel(
    grad, psum, out, pout,
    from_core, merged, qa, qb, ra, rb, total, other, all_q,
    pcore, psumc, pxy, pz,
    core_s, core_r, a_s, a_r, b_s, b_r, ag_s, ag_r, pc_s, pc_r, xy_s, xy_r, z_s, z_r,
):
    b = lax.axis_index("band")
    p = lax.axis_index("pos")
    core = lax.rem(b, 2)
    chip = b // 2
    z = lax.rem(chip, NZ)
    y = chip // NZ
    sb = b + 1 - 2 * core
    sib = {"band": sb}

    def at(dx, dy=0, **more):
        device = dict(more)
        if dx:
            device["pos"] = lax.rem(p + dx, NX)
        if dy:
            device["band"] = b + 2 * NZ * (lax.rem(y + dy, NY) - y)
        return device

    xys = [(dx, dy) for dy in range(NY) for dx in range(NX) if dx or dy]
    zdev = [None] + [{"band": b + 2 * (lax.rem(z + d, NZ) - z)} for d in range(1, NZ)]

    barrier = pltpu.get_barrier_semaphore()
    for device in [at(dx, band=sb) for dx in range(NX)] + [at(*d) for d in xys] + zdev[1:]:
        signal(barrier, device)
    for dx in range(NX):

        @pl.when(chip > 0)
        def _():
            signal(barrier, at(dx, band=b - 2))

    pl.semaphore_wait(barrier, NX + NX * NY - 1 + NZ - 1 + NX * jnp.minimum(CHIPS - 1 - chip, 1))

    first = remote(psum.at[1 - core], pcore, pc_s.at[0], pc_r.at[0], sib)
    first.start()
    piece = [lax.rem(p + dx, NX) for dx in range(NX)]
    order = (2, 1, 3, 0)
    to_core = {
        dx: remote(
            grad.at[piece[dx] // 2, 2 * (1 - core) + lax.rem(piece[dx], 2)],
            from_core.at[dx], core_s.at[dx], core_r.at[dx], sib,
        )
        for dx in order
    }
    for dx in order:
        to_core[dx].start()

    first.wait_recv()
    psumc[...] = psum[core] + pcore[...]
    xy_send = []
    for i, (dx, dy) in enumerate(xys):
        rows = pl.ds(16 * (NX * lax.rem(y + dy, NY) + lax.rem(p + dx, NX)), 16)
        xy_send.append(remote(psumc.at[rows], pxy.at[i], xy_s.at[i], xy_r.at[i], at(dx, dy)))
    for copy in xy_send:
        copy.start()

    a_send = {dx: remote(qa.at[dx], ra.at[dx], a_s.at[dx], a_r.at[dx], at(dx)) for dx in (2, 1, 3)}
    b_send = {dx: remote(qb.at[dx], rb.at[dx], b_s.at[dx], b_r.at[dx], at(dx, band=b + 2)) for dx in order}
    for dx in order:
        to_core[dx].wait_recv()
        merged[dx, pl.ds(ROWS * (1 - core), BR), :] = jnp.zeros((BR, LANES), F32)
        merged[dx, pl.ds(BR * core, ROWS), :] = grad[piece[dx] // 2, 2 * core + lax.rem(piece[dx], 2)]
        merged[dx, pl.ds(BR * (1 - core), ROWS), :] += from_core[dx]
        if dx:
            code(merged[dx, :OWN, :], qa.at[dx], OWN)
            a_send[dx].start()
        code(merged[dx, OWN:, :], qb.at[dx], BELOW)

        @pl.when(chip < CHIPS - 1)
        def _():
            b_send[dx].start()

    mine = pl.ds(16 * (NX * y + p), 16)
    for copy in xy_send:
        copy.wait_recv()
    part = psumc[mine, :]
    for i in range(len(xys)):
        part = part + pxy[i]
    pz[z] = part
    z_send = [remote(pz.at[z], pz.at[z], z_s.at[d], z_r.at[d], zdev[d]) for d in range(1, NZ)]
    for copy in z_send:
        copy.start()

    for dx in (1, 3, 2):
        a_send[dx].wait_recv()
    total[...] = merged[0, :OWN, :] + (decode(ra.at[1], OWN) + decode(ra.at[3], OWN) + decode(ra.at[2], OWN))

    @pl.when(chip > 0)
    def _():
        for dx in order:
            b_send[dx].wait_recv()
        total[:BELOW, :] += (decode(rb.at[0], BELOW) + decode(rb.at[1], BELOW)) + (
            decode(rb.at[2], BELOW) + decode(rb.at[3], BELOW)
        )

    slot = NX * core + p
    code(total[pl.ds(BR * (1 - core), BR), :], other, BR)
    code(total[pl.ds(BR * core, BR), :], all_q.at[slot], BR)
    gather = [
        remote(all_q.at[slot], all_q.at[slot], ag_s.at[dx], ag_r.at[dx], at(dx)) for dx in range(1, NX)
    ] + [remote(other, all_q.at[slot], ag_s.at[NX + dx], ag_r.at[NX + dx], at(dx, band=sb)) for dx in range(NX)]
    for copy in gather:
        copy.start()

    for copy in z_send:
        copy.wait_recv()
    part = ((pz[0] + pz[1]) + (pz[2] + pz[3])) + ((pz[4] + pz[5]) + (pz[6] + pz[7]))
    pout[core, mine, :] = part * F32(1.0 / math.sqrt(LIVE))
    xy_back = [
        remote(pout.at[core, mine], pout.at[core, mine], xy_s.at[16 + i], xy_r.at[16 + i], at(dx, dy))
        for i, (dx, dy) in enumerate(xys)
    ]
    for copy in xy_back:
        copy.start()

    for copy in gather:
        copy.wait_recv()
    for c in range(2):
        for j in range(NX):
            block = 2 * c + j % 2
            out[j // 2, :, block * LANES : (block + 1) * LANES] = decode(all_q.at[NX * c + j], BR)

    for copy in xy_back:
        copy.wait_recv()
    last = remote(pout.at[core], pout.at[core], pc_s.at[1], pc_r.at[1], sib)
    last.start()
    last.wait_recv()

    for copy in [first, last] + list(to_core.values()) + xy_send + list(a_send.values()) + z_send + gather + xy_back:
        copy.wait_send()

    @pl.when(chip < CHIPS - 1)
    def _():
        for copy in b_send.values():
            copy.wait_send()


VM = pl.BlockSpec(memory_space=pltpu.VMEM)
SM = pl.BlockSpec(memory_space=pltpu.SMEM)
HBM = pl.BlockSpec(memory_space=pltpu.HBM)
DMA = pltpu.SemaphoreType.DMA


def params(cid=None):
    return pltpu.CompilerParams(vmem_limit_bytes=40 << 20, collective_id=cid, has_side_effects=cid is not None)


def halo(obj, waves, probe, measured, rows, cols):
    return pl.pallas_call(
        halo_kernel,
        out_shape=(
            jax.ShapeDtypeStruct((2, BLOCKS, ROWS, LANES), F32),
            jax.ShapeDtypeStruct((2 * W, 2 * W), BF16),
            jax.ShapeDtypeStruct((2 * W, 2 * W), BF16),
            jax.ShapeDtypeStruct(probe.shape, probe.dtype),
            jax.ShapeDtypeStruct(measured.shape, measured.dtype),
            jax.ShapeDtypeStruct(rows.shape, rows.dtype),
            jax.ShapeDtypeStruct(cols.shape, cols.dtype),
        ),
        in_specs=[HBM] * 6,
        out_specs=(VM, VM, VM, VM, VM, SM, SM),
        scratch_shapes=[
            pltpu.VMEM((2, BR, NCOLS), F32),
            pltpu.VMEM((W, 2 * W), F32),
            pltpu.VMEM((2, BR, NCOLS), BF16),
            pltpu.VMEM((2, BR, NCOLS), BF16),
            pltpu.VMEM((2, TAIL, NCOLS), BF16),
            DMA((2, 2)),
            DMA((2, 2)),
            DMA((7,)),
        ],
        compiler_params=params(0),
        name="halo",
    )(obj, waves, probe, measured, rows, cols)


def slots(counts, rows, cols, win, probe, measured, left, right):
    return pl.pallas_call(
        slots_kernel,
        out_shape=(
            jax.ShapeDtypeStruct((2, BLOCKS, ROWS, LANES), F32),
            jax.ShapeDtypeStruct((2, W, W), F32),
        ),
        in_specs=[SM, SM, SM, VM, VM, VM, VM, VM],
        out_specs=(VM, VM),
        compiler_params=params(),
        name="slots",
    )(counts, rows, cols, win, probe, measured, left, right)


def merge(grad, psum):
    coded = lambda n, *lead: pltpu.VMEM((*lead, n + EXTRA, LANES), jnp.int16)
    piece = lambda n, *lead: pltpu.VMEM((*lead, n, LANES), F32)
    flat = lambda n, *lead: pltpu.VMEM((*lead, n, W), F32)
    return pl.pallas_call(
        merge_kernel,
        out_shape=(
            jax.ShapeDtypeStruct((2, BR, NCOLS), F32),
            jax.ShapeDtypeStruct((2, W, W), F32),
        ),
        in_specs=[VM, VM],
        out_specs=(VM, VM),
        scratch_shapes=[
            piece(ROWS, NX), piece(CHIP, NX),
            coded(OWN, NX), coded(BELOW, NX), coded(OWN, NX), coded(BELOW, NX),
            piece(OWN), coded(BR), coded(BR, 2 * NX),
            flat(W), flat(W), flat(16, 15), flat(16, NZ),
        ]
        + [DMA((NX,))] * 6
        + [DMA((2 * NX,))] * 2
        + [DMA((2,))] * 2
        + [DMA((32,))] * 2
        + [DMA((NZ,))] * 2,
        compiler_params=params(1),
        name="merge",
    )(grad, psum)


def on_device(object_field, probe, measured, row_offset, col_offset, counts):
    win, left, right, probe, measured, rows, cols = halo(
        *[
            pltpu.with_memory_space_constraint(v, pltpu.HBM)
            for v in (object_field, jnp.asarray(table()), probe, measured, row_offset, col_offset)
        ]
    )
    grad, psum = slots(counts, rows, cols, win, probe, measured, left, right)
    return merge(grad, psum)


def solution(mesh):
    placed = (
        P(None, "band", None),
        P(),
        P(("band", "pos"), None, None),
        P(("band", "pos")),
        P(("band", "pos")),
        P(("band", "pos")),
    )
    return jax.shard_map(
        on_device,
        mesh=mesh,
        in_specs=placed,
        out_specs=(P(None, "band", None), P()),
        check_vma=False,
    )
```

```python
import math

import jax
import jax.numpy as jnp
import ml_dtypes
import numpy as np
from jax import lax
from jax.experimental import pallas as pl
from jax.experimental.pallas import tpu as pltpu
from jax.sharding import PartitionSpec as P

W = 256
BR = 192
NCOLS = 512
CAP = 12
GROUP = 6
LIVE = 1024
LANES = 128
BLOCKS = NCOLS // LANES
TAIL = 64
ROWS = 2 * BR + TAIL
OWN = 2 * BR
BELOW = BR + TAIL
CHIP = OWN + BELOW
EXTRA = 16
TINY = 1e-33
FULL = 16000.0
NX, NY, NZ = 4, 4, 8
CHIPS = NY * NZ
BANDS = 2 * CHIPS
F32 = jnp.float32
BF16 = jnp.bfloat16
MESH = pl.DeviceIdType.MESH


def table():
    index = np.arange(W, dtype=np.int32)
    phase = index[:, None] * index[None, :] % W
    angle = phase.astype(np.float32) * np.float32(2.0 * math.pi / W)
    factor = np.float32(1.0 / math.sqrt(W))
    real = (np.cos(angle) * factor).astype(ml_dtypes.bfloat16)
    imag = (-np.sin(angle) * factor).astype(ml_dtypes.bfloat16)
    return np.concatenate([real, imag], 1).astype(np.float32)


def dot(a, b):
    return jnp.dot(a, b, preferred_element_type=F32)


def remote(src, dst, send, recv, device):
    return pltpu.make_async_remote_copy(
        src_ref=src, dst_ref=dst, send_sem=send, recv_sem=recv, device_id=device, device_id_type=MESH
    )


def signal(barrier, device):
    pl.semaphore_signal(barrier, inc=1, device_id=device, device_id_type=MESH)


def halo_kernel(
    obj, table, probe_in, meas_in, row_in, col_in,
    win, left, right, probe, meas, row, col,
    own, waves, low, near, far, send, recv, load,
):
    b = lax.axis_index("band")
    barrier = pltpu.get_barrier_semaphore()
    for step in (1, 2):

        @pl.when(b + step < BANDS)
        def _():
            signal(barrier, {"band": b + step})

    loads = [pltpu.make_async_copy(obj.at[plane], own.at[plane], load.at[plane]) for plane in range(2)]
    rest = ((table, waves), (row_in, row), (col_in, col), (probe_in, probe), (meas_in, meas))
    loads += [pltpu.make_async_copy(src, dst, load.at[2 + i]) for i, (src, dst) in enumerate(rest)]
    for copy in loads:
        copy.start()
    for plane in range(2):
        loads[plane].wait()
        low[plane] = own[plane].astype(BF16)

    def copies(step):
        src, dst = (low, near) if step == 1 else (low.at[:, :TAIL], far)
        return [
            remote(src.at[plane], dst.at[plane], send.at[step - 1, plane], recv.at[step - 1, plane], {"band": b - step})
            for plane in range(2)
        ]

    @pl.when(b > 0)
    def _():
        pl.semaphore_wait(barrier, jnp.minimum(b, 2))

    for step in (1, 2):

        @pl.when(b >= step)
        def _():
            for copy in copies(step):
                copy.start()

    loads[2].wait()
    real, imag = waves[:, :W], waves[:, W:]
    for rows, first, second in ((0, real, imag), (W, -imag, real)):
        right[rows : rows + W, :W] = first.astype(BF16)
        right[rows : rows + W, W:] = second.astype(BF16)
    for rows, first, second in ((0, real, -imag), (W, imag, real)):
        left[rows : rows + W, :W] = first.astype(BF16)
        left[rows : rows + W, W:] = second.astype(BF16)

    def fill(src, top, count):
        for plane in range(2):
            for block in range(BLOCKS):
                win[plane, block, top : top + count] = src[plane, :, block * LANES : (block + 1) * LANES].astype(F32)

    fill(low, 0, BR)
    for step, src, top, count in ((1, near, BR, BR), (2, far, 2 * BR, TAIL)):

        @pl.when(b + step < BANDS)
        def _():
            for copy in copies(step):
                copy.wait_recv()
            fill(src, top, count)

        @pl.when(b + step >= BANDS)
        def _():
            win[:, :, top : top + count] = jnp.zeros((2, BLOCKS, count, LANES), F32)

    for copy in loads[3:]:
        copy.wait()
    for step in (1, 2):

        @pl.when(b >= step)
        def _():
            for copy in copies(step):
                copy.wait_send()


def run_group(base, n, row, col, win, probe, meas, left, right, psum, put):
    lane = lax.broadcasted_iota(jnp.int32, (W, LANES), 1)
    place, patches, half, resid, spread, chi = ({} for _ in range(6))

    def enter(k):
        s = base + k
        c = col[s]
        block = jnp.where(c >= LANES, 1, 0)
        place[k] = (row[s], block, c - LANES * block)
        r, block, shift = place[k]
        back = lax.rem(LANES - shift, LANES)
        head = lane < LANES - shift
        patch = []
        for plane in range(2):
            parts = [pltpu.roll(win[plane, block + j, pl.ds(r, W), :], back, 1) for j in range(3)]
            patch.append(
                jnp.concatenate([jnp.where(head, parts[0], parts[1]), jnp.where(head, parts[1], parts[2])], 1)
            )
        patches[k] = patch
        pr, pi = patch
        qr, qi = probe[0], probe[1]
        exit_wave = jnp.concatenate([qr * pr - qi * pi, qr * pi + qi * pr], 0).astype(BF16)
        half[k] = dot(left[...], exit_wave).astype(BF16)

    def detect(k):
        wave = dot(jnp.concatenate([half[k][:W], half[k][W:]], 1), right[...])
        wr, wi = wave[:, :W], wave[:, W:]
        live = jnp.where(base + k < n, F32(1.0), F32(0.0))
        excess = (wr * wr + wi * wi - meas[base + k].astype(F32)) * live
        resid[k] = jnp.concatenate([wr * excess, wi * excess], 1).astype(BF16)

    def over_columns(k):
        spread[k] = dot(resid[k], left[...]).astype(BF16)

    def over_rows(k):
        chi[k] = dot(right[...], jnp.concatenate([spread[k][:, :W], spread[k][:, W:]], 0))

    def leave(k):
        r, block, shift = place[k]
        ahead = lax.rem(shift, LANES)
        tail = lane >= shift
        pr, pi = patches[k]
        qr, qi = probe[0], probe[1]
        cr, ci = chi[k][:W], chi[k][W:]
        psum[0] += pr * cr + pi * ci
        psum[1] += pr * ci - pi * cr
        for plane, g in enumerate((qr * cr + qi * ci, qr * ci - qi * cr)):
            g0 = pltpu.roll(g[:, :LANES], ahead, 1)
            g1 = pltpu.roll(g[:, LANES:], ahead, 1)
            parts = jnp.where(tail, g0, 0.0), jnp.where(tail, g1, g0), jnp.where(tail, 0.0, g1)
            put(k, plane, r, block, parts)

    stages = (enter, detect, over_columns, over_rows, leave)
    for t in range(GROUP + len(stages) - 1):
        for at in reversed(range(len(stages))):
            if 0 <= t - at < GROUP:
                stages[at](t - at)


def slots_kernel(cnt, row, col, win, probe, meas, left, right, grad, psum):
    grad[...] = jnp.zeros_like(grad)
    psum[...] = jnp.zeros_like(psum)
    n = cnt[0]

    def put(k, plane, r, block, parts):
        for j, part in enumerate(parts):
            grad[plane, block + j, pl.ds(r, W), :] += part

    def group(i, carry):
        run_group(GROUP * (i + 1), n, row, col, win, probe, meas, left, right, psum, put)
        return carry

    lax.fori_loop(0, (n - 1) // GROUP, group, 0)


def signed_power(value):
    most = jnp.maximum(jnp.max(jnp.abs(value), axis=0, keepdims=True), F32(TINY))
    return jnp.floor(jnp.log2(most))


def code(value, dst, rows):
    power = signed_power(value)
    scaled = value * (jnp.exp2(-power) * F32(FULL))
    dst[:rows] = jnp.round(scaled).astype(jnp.int32).astype(jnp.int16)
    dst[rows:] = jnp.broadcast_to(power, (EXTRA, LANES)).astype(jnp.int32).astype(jnp.int16)


def decode(src, rows):
    power = src[rows:].astype(jnp.int32).astype(F32)[:1]
    return src[:rows].astype(jnp.int32).astype(F32) * (jnp.exp2(power) * F32(1.0 / FULL))


def merge_kernel(
    cnt, row, col, win, probe, meas, left, right, grad, psum_in, out, pout,
    spots, psum, to_core_buf, from_core, merged, qa, qb, ra, rb, total, other, all_q,
    pcore, psumc, pxy, pz,
    core_s, core_r, a_s, a_r, b_s, b_r, ag_s, ag_r, pc_s, pc_r, xy_s, xy_r, z_s, z_r,
):
    b = lax.axis_index("band")
    p = lax.axis_index("pos")
    core = lax.rem(b, 2)
    chip = b // 2
    z = lax.rem(chip, NZ)
    y = chip // NZ
    sb = b + 1 - 2 * core
    sib = {"band": sb}

    def at(dx, dy=0, **more):
        device = dict(more)
        if dx:
            device["pos"] = lax.rem(p + dx, NX)
        if dy:
            device["band"] = b + 2 * NZ * (lax.rem(y + dy, NY) - y)
        return device

    xys = [(dx, dy) for dy in range(NY) for dx in range(NX) if dx or dy]
    zdev = [None] + [{"band": b + 2 * (lax.rem(z + d, NZ) - z)} for d in range(1, NZ)]

    barrier = pltpu.get_barrier_semaphore()
    for device in [at(dx, band=sb) for dx in range(NX)] + [at(*d) for d in xys] + zdev[1:]:
        signal(barrier, device)
    for dx in range(NX):

        @pl.when(chip > 0)
        def _():
            signal(barrier, at(dx, band=b - 2))

    for k in range(GROUP):
        spots[k, :, :, :BR, :] = jnp.zeros((2, BLOCKS, BR, LANES), F32)
        spots[k, :, :, BR + W :, :] = jnp.zeros((2, BLOCKS, BR, LANES), F32)
    psum[...] = psum_in[...]
    middle = pl.ds(BR, W)

    def put(k, plane, r, block, parts):
        second = block > 0
        a, c, d = parts
        zero = jnp.zeros_like(a)
        for j, (low, high) in enumerate(((a, zero), (c, a), (d, c), (zero, d))):
            spots[k, plane, j, middle, :] = jnp.where(second, high, low)

    run_group(0, cnt[0], row, col, win, probe, meas, left, right, psum, put)

    def window(plane, block):
        total = grad[plane, block]
        for k in range(GROUP):
            total = total + spots[k, plane, block, pl.ds(BR - row[k], ROWS), :]
        return total

    pl.semaphore_wait(barrier, NX + NX * NY - 1 + NZ - 1 + NX * jnp.minimum(CHIPS - 1 - chip, 1))

    first = remote(psum.at[1 - core], pcore, pc_s.at[0], pc_r.at[0], sib)
    first.start()
    piece = [lax.rem(p + dx, NX) for dx in range(NX)]
    order = (2, 1, 3, 0)
    to_core = {
        dx: remote(to_core_buf.at[dx], from_core.at[dx], core_s.at[dx], core_r.at[dx], sib) for dx in order
    }
    for dx in order:
        to_core_buf[dx] = window(piece[dx] // 2, 2 * (1 - core) + lax.rem(piece[dx], 2))
        to_core[dx].start()

    first.wait_recv()
    psumc[...] = psum[core] + pcore[...]
    xy_send = []
    for i, (dx, dy) in enumerate(xys):
        rows = pl.ds(16 * (NX * lax.rem(y + dy, NY) + lax.rem(p + dx, NX)), 16)
        xy_send.append(remote(psumc.at[rows], pxy.at[i], xy_s.at[i], xy_r.at[i], at(dx, dy)))
    for copy in xy_send:
        copy.start()

    a_send = {dx: remote(qa.at[dx], ra.at[dx], a_s.at[dx], a_r.at[dx], at(dx)) for dx in (2, 1, 3)}
    b_send = {dx: remote(qb.at[dx], rb.at[dx], b_s.at[dx], b_r.at[dx], at(dx, band=b + 2)) for dx in order}
    for dx in order:
        merged[dx, pl.ds(ROWS * (1 - core), BR), :] = jnp.zeros((BR, LANES), F32)
        merged[dx, pl.ds(BR * core, ROWS), :] = window(piece[dx] // 2, 2 * core + lax.rem(piece[dx], 2))
        to_core[dx].wait_recv()
        merged[dx, pl.ds(BR * (1 - core), ROWS), :] += from_core[dx]
        if dx:
            code(merged[dx, :OWN, :], qa.at[dx], OWN)
            a_send[dx].start()
        code(merged[dx, OWN:, :], qb.at[dx], BELOW)

        @pl.when(chip < CHIPS - 1)
        def _():
            b_send[dx].start()

    mine = pl.ds(16 * (NX * y + p), 16)
    for copy in xy_send:
        copy.wait_recv()
    part = psumc[mine, :]
    for i in range(len(xys)):
        part = part + pxy[i]
    pz[z] = part
    z_send = [remote(pz.at[z], pz.at[z], z_s.at[d], z_r.at[d], zdev[d]) for d in range(1, NZ)]
    for copy in z_send:
        copy.start()

    for dx in (1, 3, 2):
        a_send[dx].wait_recv()
    total[...] = merged[0, :OWN, :] + (decode(ra.at[1], OWN) + decode(ra.at[3], OWN) + decode(ra.at[2], OWN))

    @pl.when(chip > 0)
    def _():
        for dx in order:
            b_send[dx].wait_recv()
        total[:BELOW, :] += (decode(rb.at[0], BELOW) + decode(rb.at[1], BELOW)) + (
            decode(rb.at[2], BELOW) + decode(rb.at[3], BELOW)
        )

    slot = NX * core + p
    code(total[pl.ds(BR * (1 - core), BR), :], other, BR)
    code(total[pl.ds(BR * core, BR), :], all_q.at[slot], BR)
    gather = [
        remote(all_q.at[slot], all_q.at[slot], ag_s.at[dx], ag_r.at[dx], at(dx)) for dx in range(1, NX)
    ] + [remote(other, all_q.at[slot], ag_s.at[NX + dx], ag_r.at[NX + dx], at(dx, band=sb)) for dx in range(NX)]
    for copy in gather:
        copy.start()

    for copy in z_send:
        copy.wait_recv()
    part = ((pz[0] + pz[1]) + (pz[2] + pz[3])) + ((pz[4] + pz[5]) + (pz[6] + pz[7]))
    pout[core, mine, :] = part * F32(1.0 / math.sqrt(LIVE))
    xy_back = [
        remote(pout.at[core, mine], pout.at[core, mine], xy_s.at[16 + i], xy_r.at[16 + i], at(dx, dy))
        for i, (dx, dy) in enumerate(xys)
    ]
    for copy in xy_back:
        copy.start()

    for copy in gather:
        copy.wait_recv()
    for c in range(2):
        for j in range(NX):
            block = 2 * c + j % 2
            out[j // 2, :, block * LANES : (block + 1) * LANES] = decode(all_q.at[NX * c + j], BR)

    for copy in xy_back:
        copy.wait_recv()
    last = remote(pout.at[core], pout.at[core], pc_s.at[1], pc_r.at[1], sib)
    last.start()
    last.wait_recv()

    for copy in [first, last] + list(to_core.values()) + xy_send + list(a_send.values()) + z_send + gather + xy_back:
        copy.wait_send()

    @pl.when(chip < CHIPS - 1)
    def _():
        for copy in b_send.values():
            copy.wait_send()


VM = pl.BlockSpec(memory_space=pltpu.VMEM)
SM = pl.BlockSpec(memory_space=pltpu.SMEM)
HBM = pl.BlockSpec(memory_space=pltpu.HBM)
DMA = pltpu.SemaphoreType.DMA


def params(cid=None):
    return pltpu.CompilerParams(vmem_limit_bytes=40 << 20, collective_id=cid, has_side_effects=cid is not None)


def halo(obj, waves, probe, measured, rows, cols):
    return pl.pallas_call(
        halo_kernel,
        out_shape=(
            jax.ShapeDtypeStruct((2, BLOCKS, ROWS, LANES), F32),
            jax.ShapeDtypeStruct((2 * W, 2 * W), BF16),
            jax.ShapeDtypeStruct((2 * W, 2 * W), BF16),
            jax.ShapeDtypeStruct(probe.shape, probe.dtype),
            jax.ShapeDtypeStruct(measured.shape, measured.dtype),
            jax.ShapeDtypeStruct(rows.shape, rows.dtype),
            jax.ShapeDtypeStruct(cols.shape, cols.dtype),
        ),
        in_specs=[HBM] * 6,
        out_specs=(VM, VM, VM, VM, VM, SM, SM),
        scratch_shapes=[
            pltpu.VMEM((2, BR, NCOLS), F32),
            pltpu.VMEM((W, 2 * W), F32),
            pltpu.VMEM((2, BR, NCOLS), BF16),
            pltpu.VMEM((2, BR, NCOLS), BF16),
            pltpu.VMEM((2, TAIL, NCOLS), BF16),
            DMA((2, 2)),
            DMA((2, 2)),
            DMA((7,)),
        ],
        compiler_params=params(0),
        name="halo",
    )(obj, waves, probe, measured, rows, cols)


def slots(counts, rows, cols, win, probe, measured, left, right):
    return pl.pallas_call(
        slots_kernel,
        out_shape=(
            jax.ShapeDtypeStruct((2, BLOCKS, ROWS, LANES), F32),
            jax.ShapeDtypeStruct((2, W, W), F32),
        ),
        in_specs=[SM, SM, SM, VM, VM, VM, VM, VM],
        out_specs=(VM, VM),
        compiler_params=params(),
        name="slots",
    )(counts, rows, cols, win, probe, measured, left, right)


def merge(counts, rows, cols, win, probe, measured, left, right, grad, psum):
    coded = lambda n, *lead: pltpu.VMEM((*lead, n + EXTRA, LANES), jnp.int16)
    piece = lambda n, *lead: pltpu.VMEM((*lead, n, LANES), F32)
    flat = lambda n, *lead: pltpu.VMEM((*lead, n, W), F32)
    return pl.pallas_call(
        merge_kernel,
        out_shape=(
            jax.ShapeDtypeStruct((2, BR, NCOLS), F32),
            jax.ShapeDtypeStruct((2, W, W), F32),
        ),
        in_specs=[SM] * 3 + [VM] * 7,
        out_specs=(VM, VM),
        scratch_shapes=[
            piece(W + 2 * BR, GROUP, 2, BLOCKS), flat(W, 2),
            piece(ROWS, NX), piece(ROWS, NX), piece(CHIP, NX),
            coded(OWN, NX), coded(BELOW, NX), coded(OWN, NX), coded(BELOW, NX),
            piece(OWN), coded(BR), coded(BR, 2 * NX),
            flat(W), flat(W), flat(16, 15), flat(16, NZ),
        ]
        + [DMA((NX,))] * 6
        + [DMA((2 * NX,))] * 2
        + [DMA((2,))] * 2
        + [DMA((32,))] * 2
        + [DMA((NZ,))] * 2,
        compiler_params=params(1),
        name="merge",
    )(counts, rows, cols, win, probe, measured, left, right, grad, psum)


def on_device(object_field, probe, measured, row_offset, col_offset, counts):
    win, left, right, probe, measured, rows, cols = halo(
        *[
            pltpu.with_memory_space_constraint(v, pltpu.HBM)
            for v in (object_field, jnp.asarray(table()), probe, measured, row_offset, col_offset)
        ]
    )
    grad, psum = slots(counts, rows, cols, win, probe, measured, left, right)
    return merge(counts, rows, cols, win, probe, measured, left, right, grad, psum)


def solution(mesh):
    placed = (
        P(None, "band", None),
        P(),
        P(("band", "pos"), None, None),
        P(("band", "pos")),
        P(("band", "pos")),
        P(("band", "pos")),
    )
    return jax.shard_map(
        on_device,
        mesh=mesh,
        in_specs=placed,
        out_specs=(P(None, "band", None), P()),
        check_vma=False,
    )
```

```python
import math

import jax
import jax.numpy as jnp
import ml_dtypes
import numpy as np
from jax import lax
from jax.experimental import pallas as pl
from jax.experimental.pallas import tpu as pltpu
from jax.sharding import PartitionSpec as P

W = 256
BR = 192
NCOLS = 512
CAP = 12
GROUP = 6
LIVE = 1024
LANES = 128
BLOCKS = NCOLS // LANES
TAIL = 64
ROWS = 2 * BR + TAIL
OWN = 2 * BR
BELOW = BR + TAIL
CHIP = OWN + BELOW
EXTRA = 16
TINY = 1e-33
FULL = 16000.0
NX, NY, NZ = 4, 4, 8
CHIPS = NY * NZ
BANDS = 2 * CHIPS
F32 = jnp.float32
BF16 = jnp.bfloat16
MESH = pl.DeviceIdType.MESH


def table():
    index = np.arange(W, dtype=np.int32)
    phase = index[:, None] * index[None, :] % W
    angle = phase.astype(np.float32) * np.float32(2.0 * math.pi / W)
    factor = np.float32(1.0 / math.sqrt(W))
    real = (np.cos(angle) * factor).astype(ml_dtypes.bfloat16)
    imag = (-np.sin(angle) * factor).astype(ml_dtypes.bfloat16)
    return np.concatenate([real, imag], 1).astype(np.float32)


def dot(a, b):
    return jnp.dot(a, b, preferred_element_type=F32)


def remote(src, dst, send, recv, device):
    return pltpu.make_async_remote_copy(
        src_ref=src, dst_ref=dst, send_sem=send, recv_sem=recv, device_id=device, device_id_type=MESH
    )


def signal(barrier, device):
    pl.semaphore_signal(barrier, inc=1, device_id=device, device_id_type=MESH)


def halo_kernel(
    obj, table, probe_in, meas_in, row_in, col_in,
    win, left, right, probe, meas, row, col,
    own, waves, low, near, far, send, recv, load,
):
    b = lax.axis_index("band")
    odd = lax.rem(b, 2)
    barrier = pltpu.get_barrier_semaphore()

    @pl.when(b + 1 < BANDS)
    def _():
        signal(barrier, {"band": b + 1})

    @pl.when((odd == 1) & (b + 2 < BANDS))
    def _():
        signal(barrier, {"band": b + 2})

    loads = [pltpu.make_async_copy(obj.at[plane], own.at[plane], load.at[plane]) for plane in range(2)]
    rest = ((table, waves), (row_in, row), (col_in, col), (probe_in, probe), (meas_in, meas))
    loads += [pltpu.make_async_copy(src, dst, load.at[2 + i]) for i, (src, dst) in enumerate(rest)]
    for copy in loads:
        copy.start()
    for plane in range(2):
        loads[plane].wait()
        low[plane] = own[plane].astype(BF16)

    head, rest_rows = pl.ds(0, TAIL), pl.ds(TAIL, BR - TAIL)
    above = [
        remote(low.at[:, rows], near.at[:, rows], send.at[i], recv.at[i], {"band": b - 1})
        for i, rows in enumerate((head, rest_rows))
    ]
    skip = remote(low.at[:, head], far, send.at[2], recv.at[2], {"band": b - 2})
    relay = remote(near.at[:, head], far, send.at[3], recv.at[2], {"band": b - 1})

    @pl.when(b > 0)
    def _():
        pl.semaphore_wait(barrier, jnp.where((odd == 1) & (b > 2), 2, 1))

    @pl.when((odd == 1) & (b > 2))
    def _():
        skip.start()

    @pl.when(b > 0)
    def _():
        for copy in above:
            copy.start()

    loads[2].wait()
    real, imag = waves[:, :W], waves[:, W:]
    for rows, first, second in ((0, real, imag), (W, -imag, real)):
        right[rows : rows + W, :W] = first.astype(BF16)
        right[rows : rows + W, W:] = second.astype(BF16)
    for rows, first, second in ((0, real, -imag), (W, imag, real)):
        left[rows : rows + W, :W] = first.astype(BF16)
        left[rows : rows + W, W:] = second.astype(BF16)

    def fill(src, top, count):
        for plane in range(2):
            for block in range(BLOCKS):
                win[plane, block, top : top + count] = src[plane, :, block * LANES : (block + 1) * LANES].astype(F32)

    fill(low, 0, BR)

    @pl.when(b + 1 < BANDS)
    def _():
        above[0].wait_recv()

        @pl.when(odd == 1)
        def _():
            relay.start()

        fill(near.at[:, head], BR, TAIL)
        above[1].wait_recv()
        fill(near.at[:, rest_rows], BR + TAIL, BR - TAIL)

    @pl.when(b + 1 >= BANDS)
    def _():
        win[:, :, BR : 2 * BR] = jnp.zeros((2, BLOCKS, BR, LANES), F32)

    @pl.when(b + 2 < BANDS)
    def _():
        skip.wait_recv()
        fill(far, 2 * BR, TAIL)

    @pl.when(b + 2 >= BANDS)
    def _():
        win[:, :, 2 * BR :] = jnp.zeros((2, BLOCKS, TAIL, LANES), F32)

    for copy in loads[3:]:
        copy.wait()

    @pl.when(b > 0)
    def _():
        for copy in above:
            copy.wait_send()

    @pl.when((odd == 1) & (b > 2))
    def _():
        skip.wait_send()

    @pl.when((odd == 1) & (b + 1 < BANDS))
    def _():
        relay.wait_send()


def run_group(base, n, row, col, win, probe, meas, left, right, psum, put):
    lane = lax.broadcasted_iota(jnp.int32, (W, LANES), 1)
    place, patches, half, resid, spread, chi = ({} for _ in range(6))

    def enter(k):
        s = base + k
        c = col[s]
        block = jnp.where(c >= LANES, 1, 0)
        place[k] = (row[s], block, c - LANES * block)
        r, block, shift = place[k]
        back = lax.rem(LANES - shift, LANES)
        head = lane < LANES - shift
        patch = []
        for plane in range(2):
            parts = [pltpu.roll(win[plane, block + j, pl.ds(r, W), :], back, 1) for j in range(3)]
            patch.append(
                jnp.concatenate([jnp.where(head, parts[0], parts[1]), jnp.where(head, parts[1], parts[2])], 1)
            )
        patches[k] = patch
        pr, pi = patch
        qr, qi = probe[0], probe[1]
        exit_wave = jnp.concatenate([qr * pr - qi * pi, qr * pi + qi * pr], 0).astype(BF16)
        half[k] = dot(left[...], exit_wave).astype(BF16)

    def detect(k):
        wave = dot(jnp.concatenate([half[k][:W], half[k][W:]], 1), right[...])
        wr, wi = wave[:, :W], wave[:, W:]
        live = jnp.where(base + k < n, F32(1.0), F32(0.0))
        excess = (wr * wr + wi * wi - meas[base + k].astype(F32)) * live
        resid[k] = jnp.concatenate([wr * excess, wi * excess], 1).astype(BF16)

    def over_columns(k):
        spread[k] = dot(resid[k], left[...]).astype(BF16)

    def over_rows(k):
        chi[k] = dot(right[...], jnp.concatenate([spread[k][:, :W], spread[k][:, W:]], 0))

    def leave(k):
        r, block, shift = place[k]
        ahead = lax.rem(shift, LANES)
        tail = lane >= shift
        pr, pi = patches[k]
        qr, qi = probe[0], probe[1]
        cr, ci = chi[k][:W], chi[k][W:]
        psum[0] += pr * cr + pi * ci
        psum[1] += pr * ci - pi * cr
        for plane, g in enumerate((qr * cr + qi * ci, qr * ci - qi * cr)):
            g0 = pltpu.roll(g[:, :LANES], ahead, 1)
            g1 = pltpu.roll(g[:, LANES:], ahead, 1)
            parts = jnp.where(tail, g0, 0.0), jnp.where(tail, g1, g0), jnp.where(tail, 0.0, g1)
            put(k, plane, r, block, parts)

    stages = (enter, detect, over_columns, over_rows, leave)
    for t in range(GROUP + len(stages) - 1):
        for at in reversed(range(len(stages))):
            if 0 <= t - at < GROUP:
                stages[at](t - at)


def slots_kernel(cnt, row, col, win, probe, meas, left, right, grad, psum):
    grad[...] = jnp.zeros_like(grad)
    psum[...] = jnp.zeros_like(psum)
    n = cnt[0]

    def put(k, plane, r, block, parts):
        for j, part in enumerate(parts):
            grad[plane, block + j, pl.ds(r, W), :] += part

    def group(i, carry):
        run_group(GROUP * (i + 1), n, row, col, win, probe, meas, left, right, psum, put)
        return carry

    lax.fori_loop(0, (n - 1) // GROUP, group, 0)


def signed_power(value):
    most = jnp.maximum(jnp.max(jnp.abs(value), axis=0, keepdims=True), F32(TINY))
    return jnp.floor(jnp.log2(most))


def code(value, dst, rows):
    power = signed_power(value)
    scaled = value * (jnp.exp2(-power) * F32(FULL))
    dst[:rows] = jnp.round(scaled).astype(jnp.int32).astype(jnp.int16)
    dst[rows:] = jnp.broadcast_to(power, (EXTRA, LANES)).astype(jnp.int32).astype(jnp.int16)


def decode(src, rows):
    power = src[rows:].astype(jnp.int32).astype(F32)[:1]
    return src[:rows].astype(jnp.int32).astype(F32) * (jnp.exp2(power) * F32(1.0 / FULL))


def merge_kernel(
    cnt, row, col, win, probe, meas, left, right, grad, psum_in, all_q, pout,
    spots, psum, to_core_buf, from_core, merged, qa, qb, ra, rb, total, other,
    pcore, psumc, pxy, pz,
    core_s, core_r, a_s, a_r, b_s, b_r, ag_s, ag_r, pc_s, pc_r, xy_s, xy_r, z_s, z_r,
):
    b = lax.axis_index("band")
    p = lax.axis_index("pos")
    core = lax.rem(b, 2)
    chip = b // 2
    z = lax.rem(chip, NZ)
    y = chip // NZ
    sb = b + 1 - 2 * core
    sib = {"band": sb}

    def at(dx, dy=0, **more):
        device = dict(more)
        if dx:
            device["pos"] = lax.rem(p + dx, NX)
        if dy:
            device["band"] = b + 2 * NZ * (lax.rem(y + dy, NY) - y)
        return device

    xys = [(dx, dy) for dy in range(NY) for dx in range(NX) if dx or dy]
    zdev = [None] + [{"band": b + 2 * (lax.rem(z + d, NZ) - z)} for d in range(1, NZ)]

    barrier = pltpu.get_barrier_semaphore()
    for device in [at(dx, band=sb) for dx in range(NX)] + [at(*d) for d in xys] + zdev[1:]:
        signal(barrier, device)
    for dx in range(NX):

        @pl.when(chip > 0)
        def _():
            signal(barrier, at(dx, band=b - 2))

    for k in range(GROUP):
        spots[k, :, :, :BR, :] = jnp.zeros((2, BLOCKS, BR, LANES), F32)
        spots[k, :, :, BR + W :, :] = jnp.zeros((2, BLOCKS, BR, LANES), F32)
    psum[...] = psum_in[...]
    middle = pl.ds(BR, W)

    def put(k, plane, r, block, parts):
        second = block > 0
        a, c, d = parts
        zero = jnp.zeros_like(a)
        for j, (low, high) in enumerate(((a, zero), (c, a), (d, c), (zero, d))):
            spots[k, plane, j, middle, :] = jnp.where(second, high, low)

    run_group(0, cnt[0], row, col, win, probe, meas, left, right, psum, put)

    def window(plane, block):
        total = grad[plane, block]
        for k in range(GROUP):
            total = total + spots[k, plane, block, pl.ds(BR - row[k], ROWS), :]
        return total

    pl.semaphore_wait(barrier, NX + NX * NY - 1 + NZ - 1 + NX * jnp.minimum(CHIPS - 1 - chip, 1))

    first = remote(psum.at[1 - core], pcore, pc_s.at[0], pc_r.at[0], sib)
    first.start()
    piece = [lax.rem(p + dx, NX) for dx in range(NX)]
    order = (2, 1, 3, 0)
    to_core = {
        dx: remote(to_core_buf.at[dx], from_core.at[dx], core_s.at[dx], core_r.at[dx], sib) for dx in order
    }
    for dx in order:
        to_core_buf[dx] = window(piece[dx] // 2, 2 * (1 - core) + lax.rem(piece[dx], 2))
        to_core[dx].start()

    first.wait_recv()
    psumc[...] = psum[core] + pcore[...]
    xy_send = []
    for i, (dx, dy) in enumerate(xys):
        rows = pl.ds(16 * (NX * lax.rem(y + dy, NY) + lax.rem(p + dx, NX)), 16)
        xy_send.append(remote(psumc.at[rows], pxy.at[i], xy_s.at[0], xy_r.at[0], at(dx, dy)))
    for copy in xy_send:
        copy.start()

    a_send = {dx: remote(qa.at[dx], ra.at[dx], a_s.at[0], a_r.at[0], at(dx)) for dx in (2, 1, 3)}
    b_send = {dx: remote(qb.at[dx], rb.at[dx], b_s.at[0], b_r.at[0], at(dx, band=b + 2)) for dx in order}
    for dx in order:
        merged[dx, pl.ds(ROWS * (1 - core), BR), :] = jnp.zeros((BR, LANES), F32)
        merged[dx, pl.ds(BR * core, ROWS), :] = window(piece[dx] // 2, 2 * core + lax.rem(piece[dx], 2))
        to_core[dx].wait_recv()
        merged[dx, pl.ds(BR * (1 - core), ROWS), :] += from_core[dx]
        if dx:
            code(merged[dx, :OWN, :], qa.at[dx], OWN)
            a_send[dx].start()
        code(merged[dx, OWN:, :], qb.at[dx], BELOW)

        @pl.when(chip < CHIPS - 1)
        def _():
            b_send[dx].start()

    mine = pl.ds(16 * (NX * y + p), 16)
    xy_all = remote(pxy, pxy, xy_s.at[0], xy_r.at[0], sib)
    xy_all.wait_recv()
    part = psumc[mine, :]
    for i in range(len(xys)):
        part = part + pxy[i]
    pz[z] = part
    z_send = [remote(pz.at[z], pz.at[z], z_s.at[0], z_r.at[0], zdev[d]) for d in range(1, NZ)]
    for copy in z_send:
        copy.start()

    for copy in [first, xy_all] + list(to_core.values()):
        copy.wait_send()
    a_all = remote(ra.at[pl.ds(1, NX - 1)], ra.at[pl.ds(1, NX - 1)], a_s.at[0], a_r.at[0], sib)
    b_all = remote(rb, rb, b_s.at[0], b_r.at[0], sib)
    a_all.wait_recv()
    total[...] = merged[0, :OWN, :] + (decode(ra.at[1], OWN) + decode(ra.at[3], OWN) + decode(ra.at[2], OWN))

    @pl.when(chip > 0)
    def _():
        b_all.wait_recv()
        total[:BELOW, :] += (decode(rb.at[0], BELOW) + decode(rb.at[1], BELOW)) + (
            decode(rb.at[2], BELOW) + decode(rb.at[3], BELOW)
        )

    slot = NX * core + p
    code(total[pl.ds(BR * (1 - core), BR), :], other, BR)
    code(total[pl.ds(BR * core, BR), :], all_q.at[slot], BR)
    gather = [remote(all_q.at[slot], all_q.at[slot], ag_s.at[0], ag_r.at[0], at(dx)) for dx in range(1, NX)]
    gather += [remote(other, all_q.at[slot], ag_s.at[0], ag_r.at[0], at(dx, band=sb)) for dx in range(NX)]
    for copy in gather:
        copy.start()

    z_all = remote(pz.at[pl.ds(0, NZ - 1)], pz.at[pl.ds(0, NZ - 1)], z_s.at[0], z_r.at[0], sib)
    z_all.wait_recv()
    part = ((pz[0] + pz[1]) + (pz[2] + pz[3])) + ((pz[4] + pz[5]) + (pz[6] + pz[7]))
    pout[core, mine, :] = part * F32(1.0 / math.sqrt(LIVE))
    xy_back = [
        remote(pout.at[core, mine], pout.at[core, mine], xy_s.at[1], xy_r.at[1], at(dx, dy))
        for i, (dx, dy) in enumerate(xys)
    ]
    for copy in xy_back:
        copy.start()

    for copy in (z_all, a_all):
        copy.wait_send()

    @pl.when(chip < CHIPS - 1)
    def _():
        b_all.wait_send()

    back_all = remote(pxy, pxy, xy_s.at[1], xy_r.at[1], sib)
    back_all.wait_recv()
    last = remote(pout.at[core], pout.at[core], pc_s.at[1], pc_r.at[1], sib)
    last.start()
    gather_all = remote(all_q.at[pl.ds(0, 2 * NX - 1)], all_q.at[pl.ds(0, 2 * NX - 1)], ag_s.at[0], ag_r.at[0], sib)
    gather_all.wait_recv()
    for copy in (gather_all, back_all):
        copy.wait_send()
    last.wait()


def finish_kernel(all_q, psum, out, pout, buf, sems):
    probe_copy = pltpu.make_async_copy(psum, pout, sems.at[2])
    probe_copy.start()
    copies = []
    for plane in range(2):
        for c in range(2):
            for j in range(2):
                block = 2 * c + j
                cols = slice(block * LANES, (block + 1) * LANES)
                buf[plane, :, cols] = decode(all_q.at[NX * c + 2 * plane + j], BR)
        copies.append(pltpu.make_async_copy(buf.at[plane], out.at[plane], sems.at[plane]))
        copies[plane].start()
    for copy in copies + [probe_copy]:
        copy.wait()


VM = pl.BlockSpec(memory_space=pltpu.VMEM)
SM = pl.BlockSpec(memory_space=pltpu.SMEM)
HBM = pl.BlockSpec(memory_space=pltpu.HBM)
DMA = pltpu.SemaphoreType.DMA


def params(cid=None):
    return pltpu.CompilerParams(vmem_limit_bytes=40 << 20, collective_id=cid, has_side_effects=cid is not None)


def halo(obj, waves, probe, measured, rows, cols):
    return pl.pallas_call(
        halo_kernel,
        out_shape=(
            jax.ShapeDtypeStruct((2, BLOCKS, ROWS, LANES), F32),
            jax.ShapeDtypeStruct((2 * W, 2 * W), BF16),
            jax.ShapeDtypeStruct((2 * W, 2 * W), BF16),
            jax.ShapeDtypeStruct(probe.shape, probe.dtype),
            jax.ShapeDtypeStruct(measured.shape, measured.dtype),
            jax.ShapeDtypeStruct(rows.shape, rows.dtype),
            jax.ShapeDtypeStruct(cols.shape, cols.dtype),
        ),
        in_specs=[HBM] * 6,
        out_specs=(VM, VM, VM, VM, VM, SM, SM),
        scratch_shapes=[
            pltpu.VMEM((2, BR, NCOLS), F32),
            pltpu.VMEM((W, 2 * W), F32),
            pltpu.VMEM((2, BR, NCOLS), BF16),
            pltpu.VMEM((2, BR, NCOLS), BF16),
            pltpu.VMEM((2, TAIL, NCOLS), BF16),
            DMA((4,)),
            DMA((3,)),
            DMA((7,)),
        ],
        compiler_params=params(0),
        name="halo",
    )(obj, waves, probe, measured, rows, cols)


def slots(counts, rows, cols, win, probe, measured, left, right):
    return pl.pallas_call(
        slots_kernel,
        out_shape=(
            jax.ShapeDtypeStruct((2, BLOCKS, ROWS, LANES), F32),
            jax.ShapeDtypeStruct((2, W, W), F32),
        ),
        in_specs=[SM, SM, SM, VM, VM, VM, VM, VM],
        out_specs=(VM, VM),
        compiler_params=params(),
        name="slots",
    )(counts, rows, cols, win, probe, measured, left, right)


def merge(counts, rows, cols, win, probe, measured, left, right, grad, psum):
    coded = lambda n, *lead: pltpu.VMEM((*lead, n + EXTRA, LANES), jnp.int16)
    piece = lambda n, *lead: pltpu.VMEM((*lead, n, LANES), F32)
    flat = lambda n, *lead: pltpu.VMEM((*lead, n, W), F32)
    return pl.pallas_call(
        merge_kernel,
        out_shape=(
            jax.ShapeDtypeStruct((2 * NX, BR + EXTRA, LANES), jnp.int16),
            jax.ShapeDtypeStruct((2, W, W), F32),
        ),
        in_specs=[SM] * 3 + [VM] * 7,
        out_specs=(VM, VM),
        scratch_shapes=[
            piece(W + 2 * BR, GROUP, 2, BLOCKS), flat(W, 2),
            piece(ROWS, NX), piece(ROWS, NX), piece(CHIP, NX),
            coded(OWN, NX), coded(BELOW, NX), coded(OWN, NX), coded(BELOW, NX),
            piece(OWN), coded(BR),
            flat(W), flat(W), flat(16, 15), flat(16, NZ),
        ]
        + [DMA((NX,))] * 2
        + [DMA((1,))] * 6
        + [DMA((2,))] * 4
        + [DMA((1,))] * 2,
        compiler_params=params(1),
        name="merge",
    )(counts, rows, cols, win, probe, measured, left, right, grad, psum)


def finish(all_q, psum):
    return pl.pallas_call(
        finish_kernel,
        out_shape=(
            jax.ShapeDtypeStruct((2, BR, NCOLS), F32),
            jax.ShapeDtypeStruct((2, W, W), F32),
        ),
        in_specs=[VM, VM],
        out_specs=(HBM, HBM),
        scratch_shapes=[pltpu.VMEM((2, BR, NCOLS), F32), DMA((3,))],
        compiler_params=params(),
        name="finish",
    )(all_q, psum)


def on_device(object_field, probe, measured, row_offset, col_offset, counts):
    win, left, right, probe, measured, rows, cols = halo(
        *[
            pltpu.with_memory_space_constraint(v, pltpu.HBM)
            for v in (object_field, jnp.asarray(table()), probe, measured, row_offset, col_offset)
        ]
    )
    grad, psum = slots(counts, rows, cols, win, probe, measured, left, right)
    return finish(*merge(counts, rows, cols, win, probe, measured, left, right, grad, psum))


def solution(mesh):
    placed = (
        P(None, "band", None),
        P(),
        P(("band", "pos"), None, None),
        P(("band", "pos")),
        P(("band", "pos")),
        P(("band", "pos")),
    )
    return jax.shard_map(
        on_device,
        mesh=mesh,
        in_specs=placed,
        out_specs=(P(None, "band", None), P()),
        check_vma=False,
    )
```

```python
import math

import jax
import jax.numpy as jnp
import ml_dtypes
import numpy as np
from jax import lax
from jax.experimental import pallas as pl
from jax.experimental.pallas import tpu as pltpu
from jax.sharding import PartitionSpec as P

W = 256
BR = 192
NCOLS = 512
CAP = 12
GROUP = 6
LIVE = 1024
LANES = 128
BLOCKS = NCOLS // LANES
TAIL = 64
ROWS = 2 * BR + TAIL
OWN = 2 * BR
BELOW = BR + TAIL
CHIP = OWN + BELOW
EXTRA = 16
TINY = 1e-33
FULL = 16000.0
NX, NY, NZ = 4, 4, 8
CHIPS = NY * NZ
BANDS = 2 * CHIPS
F32 = jnp.float32
BF16 = jnp.bfloat16
MESH = pl.DeviceIdType.MESH


def table():
    index = np.arange(W, dtype=np.int32)
    phase = index[:, None] * index[None, :] % W
    angle = phase.astype(np.float32) * np.float32(2.0 * math.pi / W)
    factor = np.float32(1.0 / math.sqrt(W))
    real = (np.cos(angle) * factor).astype(ml_dtypes.bfloat16)
    imag = (-np.sin(angle) * factor).astype(ml_dtypes.bfloat16)
    return np.concatenate([real, imag], 1).astype(np.float32)


def dot(a, b):
    return jnp.dot(a, b, preferred_element_type=F32)


def remote(src, dst, send, recv, device):
    return pltpu.make_async_remote_copy(
        src_ref=src, dst_ref=dst, send_sem=send, recv_sem=recv, device_id=device, device_id_type=MESH
    )


def signal(barrier, device):
    pl.semaphore_signal(barrier, inc=1, device_id=device, device_id_type=MESH)


def halo_kernel(
    obj, table, probe_in, meas_in, row_in, col_in,
    win, left, right, probe, meas, row, col,
    own, waves, low, near, far, send, recv, load,
):
    b = lax.axis_index("band")
    odd = lax.rem(b, 2)
    barrier = pltpu.get_barrier_semaphore()

    @pl.when(b + 1 < BANDS)
    def _():
        signal(barrier, {"band": b + 1})

    @pl.when((odd == 1) & (b + 2 < BANDS))
    def _():
        signal(barrier, {"band": b + 2})

    loads = [pltpu.make_async_copy(obj.at[plane], own.at[plane], load.at[plane]) for plane in range(2)]
    rest = ((table, waves), (row_in, row), (col_in, col), (probe_in, probe), (meas_in, meas))
    loads += [pltpu.make_async_copy(src, dst, load.at[2 + i]) for i, (src, dst) in enumerate(rest)]
    for copy in loads:
        copy.start()
    for plane in range(2):
        loads[plane].wait()
        low[plane] = own[plane].astype(BF16)

    head, rest_rows = pl.ds(0, TAIL), pl.ds(TAIL, BR - TAIL)
    above = [
        remote(low.at[:, rows], near.at[:, rows], send.at[i], recv.at[i], {"band": b - 1})
        for i, rows in enumerate((head, rest_rows))
    ]
    skip = remote(low.at[:, head], far, send.at[2], recv.at[2], {"band": b - 2})
    relay = remote(near.at[:, head], far, send.at[3], recv.at[2], {"band": b - 1})

    @pl.when(b > 0)
    def _():
        pl.semaphore_wait(barrier, jnp.where((odd == 1) & (b > 2), 2, 1))

    @pl.when((odd == 1) & (b > 2))
    def _():
        skip.start()

    @pl.when(b > 0)
    def _():
        for copy in above:
            copy.start()

    loads[2].wait()
    real, imag = waves[:, :W], waves[:, W:]
    for rows, first, second in ((0, real, imag), (W, -imag, real)):
        right[rows : rows + W, :W] = first.astype(BF16)
        right[rows : rows + W, W:] = second.astype(BF16)
    for rows, first, second in ((0, real, -imag), (W, imag, real)):
        left[rows : rows + W, :W] = first.astype(BF16)
        left[rows : rows + W, W:] = second.astype(BF16)

    def fill(src, top, count):
        for plane in range(2):
            for block in range(BLOCKS):
                win[plane, block, top : top + count] = src[plane, :, block * LANES : (block + 1) * LANES].astype(F32)

    fill(low, 0, BR)

    @pl.when(b + 1 < BANDS)
    def _():
        above[0].wait_recv()

        @pl.when(odd == 1)
        def _():
            relay.start()

        fill(near.at[:, head], BR, TAIL)
        above[1].wait_recv()
        fill(near.at[:, rest_rows], BR + TAIL, BR - TAIL)

    @pl.when(b + 1 >= BANDS)
    def _():
        win[:, :, BR : 2 * BR] = jnp.zeros((2, BLOCKS, BR, LANES), F32)

    @pl.when(b + 2 < BANDS)
    def _():
        skip.wait_recv()
        fill(far, 2 * BR, TAIL)

    @pl.when(b + 2 >= BANDS)
    def _():
        win[:, :, 2 * BR :] = jnp.zeros((2, BLOCKS, TAIL, LANES), F32)

    for copy in loads[3:]:
        copy.wait()

    @pl.when(b > 0)
    def _():
        for copy in above:
            copy.wait_send()

    @pl.when((odd == 1) & (b > 2))
    def _():
        skip.wait_send()

    @pl.when((odd == 1) & (b + 1 < BANDS))
    def _():
        relay.wait_send()


def run_group(base, n, row, col, win, probe, meas, left, right, psum, put):
    lane = lax.broadcasted_iota(jnp.int32, (W, LANES), 1)
    place, patches, half, resid, spread, chi = ({} for _ in range(6))

    def enter(k):
        s = base + k
        c = col[s]
        block = jnp.where(c >= LANES, 1, 0)
        place[k] = (row[s], block, c - LANES * block)
        r, block, shift = place[k]
        back = lax.rem(LANES - shift, LANES)
        head = lane < LANES - shift
        patch = []
        for plane in range(2):
            parts = [pltpu.roll(win[plane, block + j, pl.ds(r, W), :], back, 1) for j in range(3)]
            patch.append(
                jnp.concatenate([jnp.where(head, parts[0], parts[1]), jnp.where(head, parts[1], parts[2])], 1)
            )
        patches[k] = patch
        pr, pi = patch
        qr, qi = probe[0], probe[1]
        exit_wave = jnp.concatenate([qr * pr - qi * pi, qr * pi + qi * pr], 0).astype(BF16)
        half[k] = dot(left[...], exit_wave).astype(BF16)

    def detect(k):
        wave = dot(jnp.concatenate([half[k][:W], half[k][W:]], 1), right[...])
        wr, wi = wave[:, :W], wave[:, W:]
        live = jnp.where(base + k < n, F32(1.0), F32(0.0))
        excess = (wr * wr + wi * wi - meas[base + k].astype(F32)) * live
        resid[k] = jnp.concatenate([wr * excess, wi * excess], 1).astype(BF16)

    def over_columns(k):
        spread[k] = dot(resid[k], left[...]).astype(BF16)

    def over_rows(k):
        chi[k] = dot(right[...], jnp.concatenate([spread[k][:, :W], spread[k][:, W:]], 0))

    def leave(k):
        r, block, shift = place[k]
        ahead = lax.rem(shift, LANES)
        tail = lane >= shift
        pr, pi = patches[k]
        qr, qi = probe[0], probe[1]
        cr, ci = chi[k][:W], chi[k][W:]
        psum[0] += pr * cr + pi * ci
        psum[1] += pr * ci - pi * cr
        for plane, g in enumerate((qr * cr + qi * ci, qr * ci - qi * cr)):
            g0 = pltpu.roll(g[:, :LANES], ahead, 1)
            g1 = pltpu.roll(g[:, LANES:], ahead, 1)
            parts = jnp.where(tail, g0, 0.0), jnp.where(tail, g1, g0), jnp.where(tail, 0.0, g1)
            put(k, plane, r, block, parts)

    stages = (enter, detect, over_columns, over_rows, leave)
    for t in range(GROUP + len(stages) - 1):
        for at in reversed(range(len(stages))):
            if 0 <= t - at < GROUP:
                stages[at](t - at)


def slots_kernel(cnt, row, col, win, probe, meas, left, right, grad, psum):
    grad[...] = jnp.zeros_like(grad)
    psum[...] = jnp.zeros_like(psum)
    n = cnt[0]

    def put(k, plane, r, block, parts):
        for j, part in enumerate(parts):
            grad[plane, block + j, pl.ds(r, W), :] += part

    def group(i, carry):
        run_group(GROUP * (i + 1), n, row, col, win, probe, meas, left, right, psum, put)
        return carry

    lax.fori_loop(0, (n - 1) // GROUP, group, 0)


def signed_power(value):
    most = jnp.maximum(jnp.max(jnp.abs(value), axis=0, keepdims=True), F32(TINY))
    return jnp.floor(jnp.log2(most))


def code(value, dst, rows):
    power = signed_power(value)
    scaled = value * (jnp.exp2(-power) * F32(FULL))
    dst[:rows] = jnp.round(scaled).astype(jnp.int32).astype(jnp.int16)
    dst[rows:] = jnp.broadcast_to(power, (EXTRA, LANES)).astype(jnp.int32).astype(jnp.int16)


def decode(src, rows, first=0, last=None):
    last = rows if last is None else last
    power = src[rows:].astype(jnp.int32).astype(F32)[:1]
    return src[first:last].astype(jnp.int32).astype(F32) * (jnp.exp2(power) * F32(1.0 / FULL))


def merge_kernel(
    cnt, row, col, win, probe, meas, left, right, grad, psum_in, all_q, pout,
    spots, psum, to_core_buf, from_core, merged, qa, qb, ra, rb, qs, rs, total, other,
    pcore, psumc, pxy, pz,
    core_s, core_r, a_s, a_r, b_s, b_r, sh_s, sh_r, ag_s, ag_r, pc_s, pc_r, xy_s, xy_r, z_s, z_r,
):
    b = lax.axis_index("band")
    p = lax.axis_index("pos")
    core = lax.rem(b, 2)
    chip = b // 2
    z = lax.rem(chip, NZ)
    y = chip // NZ
    sb = b + 1 - 2 * core
    sib = {"band": sb}

    def at(dx, dy=0, **more):
        device = dict(more)
        if dx:
            device["pos"] = lax.rem(p + dx, NX)
        if dy:
            device["band"] = b + 2 * NZ * (lax.rem(y + dy, NY) - y)
        return device

    xys = [(dx, dy) for dy in range(NY) for dx in range(NX) if dx or dy]
    zdev = [None] + [{"band": b + 2 * (lax.rem(z + d, NZ) - z)} for d in range(1, NZ)]

    barrier = pltpu.get_barrier_semaphore()
    for device in [at(dx, band=sb) for dx in range(NX)] + [at(*d) for d in xys] + zdev[1:]:
        signal(barrier, device)
    @pl.when(chip > 0)
    def _():
        signal(barrier, {"band": b - 2})

    for k in range(GROUP):
        spots[k, :, :, :BR, :] = jnp.zeros((2, BLOCKS, BR, LANES), F32)
        spots[k, :, :, BR + W :, :] = jnp.zeros((2, BLOCKS, BR, LANES), F32)
    psum[...] = psum_in[...]
    middle = pl.ds(BR, W)

    def put(k, plane, r, block, parts):
        second = block > 0
        a, c, d = parts
        zero = jnp.zeros_like(a)
        for j, (low, high) in enumerate(((a, zero), (c, a), (d, c), (zero, d))):
            spots[k, plane, j, middle, :] = jnp.where(second, high, low)

    run_group(0, cnt[0], row, col, win, probe, meas, left, right, psum, put)

    def window(plane, block):
        total = grad[plane, block]
        for k in range(GROUP):
            total = total + spots[k, plane, block, pl.ds(BR - row[k], ROWS), :]
        return total

    pl.semaphore_wait(barrier, NX + NX * NY - 1 + NZ - 1 + jnp.minimum(CHIPS - 1 - chip, 1))

    first = remote(psum.at[1 - core], pcore, pc_s.at[0], pc_r.at[0], sib)
    first.start()
    piece = [lax.rem(p + dx, NX) for dx in range(NX)]
    order = (2, 1, 3, 0)
    to_core = {
        dx: remote(to_core_buf.at[dx], from_core.at[dx], core_s.at[dx], core_r.at[dx], sib) for dx in order
    }
    for dx in order:
        to_core_buf[dx] = window(piece[dx] // 2, 2 * (1 - core) + lax.rem(piece[dx], 2))
        to_core[dx].start()

    first.wait_recv()
    psumc[...] = psum[core] + pcore[...]
    xy_send = []
    for i, (dx, dy) in enumerate(xys):
        rows = pl.ds(16 * (NX * lax.rem(y + dy, NY) + lax.rem(p + dx, NX)), 16)
        xy_send.append(remote(psumc.at[rows], pxy.at[i], xy_s.at[0], xy_r.at[0], at(dx, dy)))
    for copy in xy_send:
        copy.start()

    a_send = {dx: remote(qa.at[dx], ra.at[dx], a_s.at[0], a_r.at[0], at(dx)) for dx in (2, 1, 3)}
    b_send = {dx: remote(qb.at[dx], rb.at[dx], b_s.at[0], b_r.at[0], at(dx)) for dx in (2, 1, 3)}
    shift = remote(qs, rs, sh_s.at[0], sh_r.at[0], {"band": b + 2})
    for dx in order:
        merged[dx, pl.ds(ROWS * (1 - core), BR), :] = jnp.zeros((BR, LANES), F32)
        merged[dx, pl.ds(BR * core, ROWS), :] = window(piece[dx] // 2, 2 * core + lax.rem(piece[dx], 2))
        to_core[dx].wait_recv()
        merged[dx, pl.ds(BR * (1 - core), ROWS), :] += from_core[dx]
        if dx:
            code(merged[dx, OWN:, :], qb.at[dx], BELOW)
            b_send[dx].start()
    for dx in order[:3]:
        code(merged[dx, :OWN, :], qa.at[dx], OWN)
        a_send[dx].start()

    mine = pl.ds(16 * (NX * y + p), 16)
    xy_all = remote(pxy, pxy, xy_s.at[0], xy_r.at[0], sib)
    xy_all.wait_recv()
    part = psumc[mine, :]
    for i in range(len(xys)):
        part = part + pxy[i]
    pz[z] = part
    z_send = [remote(pz.at[z], pz.at[z], z_s.at[0], z_r.at[0], zdev[d]) for d in range(1, NZ)]
    for copy in z_send:
        copy.start()

    for copy in [first, xy_all] + list(to_core.values()):
        copy.wait_send()
    others = pl.ds(1, NX - 1)
    a_all = remote(ra.at[others], ra.at[others], a_s.at[0], a_r.at[0], sib)
    b_all = remote(rb.at[others], rb.at[others], b_s.at[0], b_r.at[0], sib)
    b_all.wait_recv()
    below = merged[0, OWN:, :] + (decode(rb.at[1], BELOW) + decode(rb.at[3], BELOW) + decode(rb.at[2], BELOW))
    code(below, qs, BELOW)

    @pl.when(chip < CHIPS - 1)
    def _():
        shift.start()

    a_all.wait_recv()
    total[...] = merged[0, :OWN, :] + (decode(ra.at[1], OWN) + decode(ra.at[3], OWN) + decode(ra.at[2], OWN))

    z_all = remote(pz.at[pl.ds(0, NZ - 1)], pz.at[pl.ds(0, NZ - 1)], z_s.at[0], z_r.at[0], sib)
    z_all.wait_recv()
    part = ((pz[0] + pz[1]) + (pz[2] + pz[3])) + ((pz[4] + pz[5]) + (pz[6] + pz[7]))
    pout[core, mine, :] = part * F32(1.0 / math.sqrt(LIVE))
    xy_back = [
        remote(pout.at[core, mine], pout.at[core, mine], xy_s.at[1], xy_r.at[1], at(dx, dy))
        for i, (dx, dy) in enumerate(xys)
    ]
    for copy in xy_back:
        copy.start()

    @pl.when(chip > 0)
    def _():
        shift.wait_recv()
        total[:BELOW, :] += decode(rs, BELOW)

    slot = NX * core + p
    code(total[pl.ds(BR * (1 - core), BR), :], other, BR)
    code(total[pl.ds(BR * core, BR), :], all_q.at[slot], BR)
    gather = [remote(all_q.at[slot], all_q.at[slot], ag_s.at[0], ag_r.at[0], at(dx)) for dx in range(1, NX)]
    gather += [remote(other, all_q.at[slot], ag_s.at[0], ag_r.at[0], at(dx, band=sb)) for dx in range(NX)]
    for copy in gather:
        copy.start()

    for copy in (z_all, a_all, b_all):
        copy.wait_send()

    @pl.when(chip < CHIPS - 1)
    def _():
        shift.wait_send()

    back_all = remote(pxy, pxy, xy_s.at[1], xy_r.at[1], sib)
    back_all.wait_recv()
    last = remote(pout.at[core], pout.at[core], pc_s.at[1], pc_r.at[1], sib)
    last.start()
    gather_all = remote(all_q.at[pl.ds(0, 2 * NX - 1)], all_q.at[pl.ds(0, 2 * NX - 1)], ag_s.at[0], ag_r.at[0], sib)
    gather_all.wait_recv()
    for copy in (gather_all, back_all):
        copy.wait_send()
    last.wait()


def finish_kernel(all_q, psum, out, pout, buf, sems):
    probe_copy = pltpu.make_async_copy(psum, pout, sems.at[2])
    probe_copy.start()
    copies = []
    for plane in range(2):
        for c in range(2):
            for j in range(2):
                block = 2 * c + j
                cols = slice(block * LANES, (block + 1) * LANES)
                buf[plane, :, cols] = decode(all_q.at[NX * c + 2 * plane + j], BR)
        copies.append(pltpu.make_async_copy(buf.at[plane], out.at[plane], sems.at[plane]))
        copies[plane].start()
    for copy in copies + [probe_copy]:
        copy.wait()


VM = pl.BlockSpec(memory_space=pltpu.VMEM)
SM = pl.BlockSpec(memory_space=pltpu.SMEM)
HBM = pl.BlockSpec(memory_space=pltpu.HBM)
DMA = pltpu.SemaphoreType.DMA


def params(cid=None):
    return pltpu.CompilerParams(vmem_limit_bytes=40 << 20, collective_id=cid, has_side_effects=cid is not None)


def halo(obj, waves, probe, measured, rows, cols):
    return pl.pallas_call(
        halo_kernel,
        out_shape=(
            jax.ShapeDtypeStruct((2, BLOCKS, ROWS, LANES), F32),
            jax.ShapeDtypeStruct((2 * W, 2 * W), BF16),
            jax.ShapeDtypeStruct((2 * W, 2 * W), BF16),
            jax.ShapeDtypeStruct(probe.shape, probe.dtype),
            jax.ShapeDtypeStruct(measured.shape, measured.dtype),
            jax.ShapeDtypeStruct(rows.shape, rows.dtype),
            jax.ShapeDtypeStruct(cols.shape, cols.dtype),
        ),
        in_specs=[HBM] * 6,
        out_specs=(VM, VM, VM, VM, VM, SM, SM),
        scratch_shapes=[
            pltpu.VMEM((2, BR, NCOLS), F32),
            pltpu.VMEM((W, 2 * W), F32),
            pltpu.VMEM((2, BR, NCOLS), BF16),
            pltpu.VMEM((2, BR, NCOLS), BF16),
            pltpu.VMEM((2, TAIL, NCOLS), BF16),
            DMA((4,)),
            DMA((3,)),
            DMA((7,)),
        ],
        compiler_params=params(0),
        name="halo",
    )(obj, waves, probe, measured, rows, cols)


def slots(counts, rows, cols, win, probe, measured, left, right):
    return pl.pallas_call(
        slots_kernel,
        out_shape=(
            jax.ShapeDtypeStruct((2, BLOCKS, ROWS, LANES), F32),
            jax.ShapeDtypeStruct((2, W, W), F32),
        ),
        in_specs=[SM, SM, SM, VM, VM, VM, VM, VM],
        out_specs=(VM, VM),
        compiler_params=params(),
        name="slots",
    )(counts, rows, cols, win, probe, measured, left, right)


def merge(counts, rows, cols, win, probe, measured, left, right, grad, psum):
    coded = lambda n, *lead: pltpu.VMEM((*lead, n + EXTRA, LANES), jnp.int16)
    piece = lambda n, *lead: pltpu.VMEM((*lead, n, LANES), F32)
    flat = lambda n, *lead: pltpu.VMEM((*lead, n, W), F32)
    return pl.pallas_call(
        merge_kernel,
        out_shape=(
            jax.ShapeDtypeStruct((2 * NX, BR + EXTRA, LANES), jnp.int16),
            jax.ShapeDtypeStruct((2, W, W), F32),
        ),
        in_specs=[SM] * 3 + [VM] * 7,
        out_specs=(VM, VM),
        scratch_shapes=[
            piece(W + 2 * BR, GROUP, 2, BLOCKS), flat(W, 2),
            piece(ROWS, NX), piece(ROWS, NX), piece(CHIP, NX),
            coded(OWN, NX), coded(BELOW, NX), coded(OWN, NX), coded(BELOW, NX), coded(BELOW), coded(BELOW),
            piece(OWN), coded(BR),
            flat(W), flat(W), flat(16, 15), flat(16, NZ),
        ]
        + [DMA((NX,))] * 2
        + [DMA((1,))] * 8
        + [DMA((2,))] * 4
        + [DMA((1,))] * 2,
        compiler_params=params(1),
        name="merge",
    )(counts, rows, cols, win, probe, measured, left, right, grad, psum)


def finish(all_q, psum):
    return pl.pallas_call(
        finish_kernel,
        out_shape=(
            jax.ShapeDtypeStruct((2, BR, NCOLS), F32),
            jax.ShapeDtypeStruct((2, W, W), F32),
        ),
        in_specs=[VM, VM],
        out_specs=(HBM, HBM),
        scratch_shapes=[pltpu.VMEM((2, BR, NCOLS), F32), DMA((3,))],
        compiler_params=params(),
        name="finish",
    )(all_q, psum)


def on_device(object_field, probe, measured, row_offset, col_offset, counts):
    win, left, right, probe, measured, rows, cols = halo(
        *[
            pltpu.with_memory_space_constraint(v, pltpu.HBM)
            for v in (object_field, jnp.asarray(table()), probe, measured, row_offset, col_offset)
        ]
    )
    grad, psum = slots(counts, rows, cols, win, probe, measured, left, right)
    return finish(*merge(counts, rows, cols, win, probe, measured, left, right, grad, psum))


def solution(mesh):
    placed = (
        P(None, "band", None),
        P(),
        P(("band", "pos"), None, None),
        P(("band", "pos")),
        P(("band", "pos")),
        P(("band", "pos")),
    )
    return jax.shard_map(
        on_device,
        mesh=mesh,
        in_specs=placed,
        out_specs=(P(None, "band", None), P()),
        check_vma=False,
    )
```

```python
import math

import jax
import jax.numpy as jnp
import ml_dtypes
import numpy as np
from jax import lax
from jax.experimental import pallas as pl
from jax.experimental.pallas import tpu as pltpu
from jax.sharding import PartitionSpec as P

W = 256
BR = 192
NCOLS = 512
CAP = 12
GROUP = 6
LIVE = 1024
LANES = 128
BLOCKS = NCOLS // LANES
TAIL = 64
ROWS = 2 * BR + TAIL
OWN = 2 * BR
BELOW = BR + TAIL
CHIP = OWN + BELOW
EXTRA = 16
TINY = 1e-33
FULL = 16000.0
NX, NY, NZ = 4, 4, 8
CHIPS = NY * NZ
BANDS = 2 * CHIPS
F32 = jnp.float32
BF16 = jnp.bfloat16
MESH = pl.DeviceIdType.MESH


def table():
    index = np.arange(W, dtype=np.int32)
    phase = index[:, None] * index[None, :] % W
    angle = phase.astype(np.float32) * np.float32(2.0 * math.pi / W)
    factor = np.float32(1.0 / math.sqrt(W))
    real = (np.cos(angle) * factor).astype(ml_dtypes.bfloat16)
    imag = (-np.sin(angle) * factor).astype(ml_dtypes.bfloat16)
    return np.concatenate([real, imag], 1).astype(np.float32)


def dot(a, b):
    return jnp.dot(a, b, preferred_element_type=F32)


def remote(src, dst, send, recv, device):
    return pltpu.make_async_remote_copy(
        src_ref=src, dst_ref=dst, send_sem=send, recv_sem=recv, device_id=device, device_id_type=MESH
    )


def signal(barrier, device):
    pl.semaphore_signal(barrier, inc=1, device_id=device, device_id_type=MESH)


def halo_kernel(
    obj, table, probe_in, meas_in, row_in, col_in,
    win, left, right, probe, meas, row, col,
    own, waves, low, near, far, send, recv, load,
):
    b = lax.axis_index("band")
    odd = lax.rem(b, 2)
    barrier = pltpu.get_barrier_semaphore()

    @pl.when(b + 1 < BANDS)
    def _():
        signal(barrier, {"band": b + 1})

    @pl.when((odd == 1) & (b + 2 < BANDS))
    def _():
        signal(barrier, {"band": b + 2})

    loads = [pltpu.make_async_copy(obj.at[plane], own.at[plane], load.at[plane]) for plane in range(2)]
    rest = ((table, waves), (row_in, row), (col_in, col), (probe_in, probe), (meas_in, meas))
    loads += [pltpu.make_async_copy(src, dst, load.at[2 + i]) for i, (src, dst) in enumerate(rest)]
    for copy in loads:
        copy.start()
    for plane in range(2):
        loads[plane].wait()
        low[plane] = own[plane].astype(BF16)

    head, rest_rows = pl.ds(0, TAIL), pl.ds(TAIL, BR - TAIL)
    above = [
        remote(low.at[:, rows], near.at[:, rows], send.at[i], recv.at[i], {"band": b - 1})
        for i, rows in enumerate((head, rest_rows))
    ]
    skip = remote(low.at[:, head], far, send.at[2], recv.at[2], {"band": b - 2})
    relay = remote(near.at[:, head], far, send.at[3], recv.at[2], {"band": b - 1})

    @pl.when(b > 0)
    def _():
        pl.semaphore_wait(barrier, jnp.where((odd == 1) & (b > 2), 2, 1))

    @pl.when((odd == 1) & (b > 2))
    def _():
        skip.start()

    @pl.when(b > 0)
    def _():
        for copy in above:
            copy.start()

    loads[2].wait()
    real, imag = waves[:, :W], waves[:, W:]
    for rows, first, second in ((0, real, imag), (W, -imag, real)):
        right[rows : rows + W, :W] = first.astype(BF16)
        right[rows : rows + W, W:] = second.astype(BF16)
    for rows, first, second in ((0, real, -imag), (W, imag, real)):
        left[rows : rows + W, :W] = first.astype(BF16)
        left[rows : rows + W, W:] = second.astype(BF16)

    def fill(src, top, count):
        for plane in range(2):
            for block in range(BLOCKS):
                win[plane, block, top : top + count] = src[plane, :, block * LANES : (block + 1) * LANES].astype(F32)

    fill(low, 0, BR)

    @pl.when(b + 1 < BANDS)
    def _():
        above[0].wait_recv()

        @pl.when(odd == 1)
        def _():
            relay.start()

        fill(near.at[:, head], BR, TAIL)
        above[1].wait_recv()
        fill(near.at[:, rest_rows], BR + TAIL, BR - TAIL)

    @pl.when(b + 1 >= BANDS)
    def _():
        win[:, :, BR : 2 * BR] = jnp.zeros((2, BLOCKS, BR, LANES), F32)

    @pl.when(b + 2 < BANDS)
    def _():
        skip.wait_recv()
        fill(far, 2 * BR, TAIL)

    @pl.when(b + 2 >= BANDS)
    def _():
        win[:, :, 2 * BR :] = jnp.zeros((2, BLOCKS, TAIL, LANES), F32)

    for copy in loads[3:]:
        copy.wait()

    @pl.when(b > 0)
    def _():
        for copy in above:
            copy.wait_send()

    @pl.when((odd == 1) & (b > 2))
    def _():
        skip.wait_send()

    @pl.when((odd == 1) & (b + 1 < BANDS))
    def _():
        relay.wait_send()


def run_group(base, n, row, col, win, probe, meas, left, right, psum, put):
    lane = lax.broadcasted_iota(jnp.int32, (W, LANES), 1)
    place, patches, half, resid, spread, chi = ({} for _ in range(6))

    def enter(k):
        s = base + k
        c = col[s]
        block = jnp.where(c >= LANES, 1, 0)
        place[k] = (row[s], block, c - LANES * block)
        r, block, shift = place[k]
        back = lax.rem(LANES - shift, LANES)
        head = lane < LANES - shift
        patch = []
        for plane in range(2):
            parts = [pltpu.roll(win[plane, block + j, pl.ds(r, W), :], back, 1) for j in range(3)]
            patch.append(
                jnp.concatenate([jnp.where(head, parts[0], parts[1]), jnp.where(head, parts[1], parts[2])], 1)
            )
        patches[k] = patch
        pr, pi = patch
        qr, qi = probe[0], probe[1]
        exit_wave = jnp.concatenate([qr * pr - qi * pi, qr * pi + qi * pr], 0).astype(BF16)
        half[k] = dot(left[...], exit_wave).astype(BF16)

    def detect(k):
        wave = dot(jnp.concatenate([half[k][:W], half[k][W:]], 1), right[...])
        wr, wi = wave[:, :W], wave[:, W:]
        live = jnp.where(base + k < n, F32(1.0), F32(0.0))
        excess = (wr * wr + wi * wi - meas[base + k].astype(F32)) * live
        resid[k] = jnp.concatenate([wr * excess, wi * excess], 1).astype(BF16)

    def over_columns(k):
        spread[k] = dot(resid[k], left[...]).astype(BF16)

    def over_rows(k):
        chi[k] = dot(right[...], jnp.concatenate([spread[k][:, :W], spread[k][:, W:]], 0))

    def leave(k):
        r, block, shift = place[k]
        ahead = lax.rem(shift, LANES)
        tail = lane >= shift
        pr, pi = patches[k]
        qr, qi = probe[0], probe[1]
        cr, ci = chi[k][:W], chi[k][W:]
        psum[0] += pr * cr + pi * ci
        psum[1] += pr * ci - pi * cr
        for plane, g in enumerate((qr * cr + qi * ci, qr * ci - qi * cr)):
            g0 = pltpu.roll(g[:, :LANES], ahead, 1)
            g1 = pltpu.roll(g[:, LANES:], ahead, 1)
            parts = jnp.where(tail, g0, 0.0), jnp.where(tail, g1, g0), jnp.where(tail, 0.0, g1)
            put(k, plane, r, block, parts)

    stages = (enter, detect, over_columns, over_rows, leave)
    for t in range(GROUP + len(stages) - 1):
        for at in reversed(range(len(stages))):
            if 0 <= t - at < GROUP:
                stages[at](t - at)


def slots_kernel(cnt, row, col, win, probe, meas, left, right, grad, psum):
    grad[...] = jnp.zeros_like(grad)
    psum[...] = jnp.zeros_like(psum)
    n = cnt[0]

    def put(k, plane, r, block, parts):
        for j, part in enumerate(parts):
            grad[plane, block + j, pl.ds(r, W), :] += part

    def group(i, carry):
        run_group(GROUP * (i + 1), n, row, col, win, probe, meas, left, right, psum, put)
        return carry

    lax.fori_loop(0, (n - 1) // GROUP, group, 0)


def signed_power(value):
    most = jnp.maximum(jnp.max(jnp.abs(value), axis=0, keepdims=True), F32(TINY))
    return jnp.floor(jnp.log2(most))


def code(value, dst, rows):
    power = signed_power(value)
    scaled = value * (jnp.exp2(-power) * F32(FULL))
    dst[:rows] = jnp.round(scaled).astype(jnp.int32).astype(jnp.int16)
    dst[rows:] = jnp.broadcast_to(power, (EXTRA, LANES)).astype(jnp.int32).astype(jnp.int16)


def decode(src, rows, first=0, last=None):
    last = rows if last is None else last
    power = src[rows:].astype(jnp.int32).astype(F32)[:1]
    return src[first:last].astype(jnp.int32).astype(F32) * (jnp.exp2(power) * F32(1.0 / FULL))


def merge_kernel(
    cnt, row, col, win, probe, meas, left, right, grad, psum_in, all_q, pout,
    spots, psum, to_core_buf, from_core, merged, qa, qb, ra, rb, qs, rs, total, other,
    pcore, psumc, pxy, pz,
    core_s, core_r, a_s, a_r, b_s, b_r, sh_s, sh_r, ag_s, ag_r, pc_s, pc_r, xy_s, xy_r, z_s, z_r,
):
    b = lax.axis_index("band")
    p = lax.axis_index("pos")
    core = lax.rem(b, 2)
    chip = b // 2
    z = lax.rem(chip, NZ)
    y = chip // NZ
    sb = b + 1 - 2 * core
    sib = {"band": sb}

    def at(dx, dy=0, **more):
        device = dict(more)
        if dx:
            device["pos"] = lax.rem(p + dx, NX)
        if dy:
            device["band"] = b + 2 * NZ * (lax.rem(y + dy, NY) - y)
        return device

    hops = (0, 1, 2, 1)
    xys = [(dx, dy) for dy in range(NY) for dx in range(NX) if dx or dy]
    xys.sort(key=lambda d: -hops[d[0]] - hops[d[1]])
    zdev = [None] + [{"band": b + 2 * (lax.rem(z + d, NZ) - z)} for d in range(1, NZ)]

    barrier = pltpu.get_barrier_semaphore()
    for device in [at(dx, band=sb) for dx in range(NX)] + [at(*d) for d in xys] + zdev[1:]:
        signal(barrier, device)
    @pl.when(chip > 0)
    def _():
        signal(barrier, {"band": b - 2})

    for k in range(GROUP):
        spots[k, :, :, :BR, :] = jnp.zeros((2, BLOCKS, BR, LANES), F32)
        spots[k, :, :, BR + W :, :] = jnp.zeros((2, BLOCKS, BR, LANES), F32)
    psum[...] = psum_in[...]
    middle = pl.ds(BR, W)

    def put(k, plane, r, block, parts):
        second = block > 0
        a, c, d = parts
        zero = jnp.zeros_like(a)
        for j, (low, high) in enumerate(((a, zero), (c, a), (d, c), (zero, d))):
            spots[k, plane, j, middle, :] = jnp.where(second, high, low)

    run_group(0, cnt[0], row, col, win, probe, meas, left, right, psum, put)

    def window(plane, block):
        total = grad[plane, block]
        for k in range(GROUP):
            total = total + spots[k, plane, block, pl.ds(BR - row[k], ROWS), :]
        return total

    pl.semaphore_wait(barrier, NX + NX * NY - 1 + NZ - 1 + jnp.minimum(CHIPS - 1 - chip, 1))

    first = remote(psum.at[1 - core], pcore, pc_s.at[0], pc_r.at[0], sib)
    first.start()
    piece = [lax.rem(p + dx, NX) for dx in range(NX)]
    order = (2, 1, 3, 0)
    to_core = {
        dx: remote(to_core_buf.at[dx], from_core.at[dx], core_s.at[dx], core_r.at[dx], sib) for dx in order
    }
    for dx in order:
        to_core_buf[dx] = window(piece[dx] // 2, 2 * (1 - core) + lax.rem(piece[dx], 2))
        to_core[dx].start()

    first.wait_recv()
    psumc[...] = psum[core] + pcore[...]
    xy_send = []
    for i, (dx, dy) in enumerate(xys):
        rows = pl.ds(16 * (NX * lax.rem(y + dy, NY) + lax.rem(p + dx, NX)), 16)
        xy_send.append(remote(psumc.at[rows], pxy.at[i], xy_s.at[0], xy_r.at[0], at(dx, dy)))
    for copy in xy_send:
        copy.start()

    a_send = {dx: remote(qa.at[dx], ra.at[dx], a_s.at[0], a_r.at[0], at(dx)) for dx in (2, 1, 3)}
    b_send = {dx: remote(qb.at[dx], rb.at[dx], b_s.at[0], b_r.at[0], at(dx)) for dx in (2, 1, 3)}
    shift = remote(qs, rs, sh_s.at[0], sh_r.at[0], {"band": b + 2})
    for dx in order:
        merged[dx, pl.ds(ROWS * (1 - core), BR), :] = jnp.zeros((BR, LANES), F32)
        merged[dx, pl.ds(BR * core, ROWS), :] = window(piece[dx] // 2, 2 * core + lax.rem(piece[dx], 2))
        to_core[dx].wait_recv()
        merged[dx, pl.ds(BR * (1 - core), ROWS), :] += from_core[dx]
        if dx:
            code(merged[dx, OWN:, :], qb.at[dx], BELOW)
            b_send[dx].start()
    for dx in order[:3]:
        code(merged[dx, :OWN, :], qa.at[dx], OWN)
        a_send[dx].start()

    mine = pl.ds(16 * (NX * y + p), 16)
    xy_all = remote(pxy, pxy, xy_s.at[0], xy_r.at[0], sib)
    xy_all.wait_recv()
    part = psumc[mine, :]
    for i in range(len(xys)):
        part = part + pxy[i]
    pz[z] = part
    z_send = [remote(pz.at[z], pz.at[z], z_s.at[0], z_r.at[0], zdev[d]) for d in (4, 3, 5, 2, 6, 1, 7)]
    for copy in z_send:
        copy.start()

    for copy in [first, xy_all] + list(to_core.values()):
        copy.wait_send()
    others = pl.ds(1, NX - 1)
    a_all = remote(ra.at[others], ra.at[others], a_s.at[0], a_r.at[0], sib)
    b_all = remote(rb.at[others], rb.at[others], b_s.at[0], b_r.at[0], sib)
    b_all.wait_recv()
    below = merged[0, OWN:, :] + (decode(rb.at[1], BELOW) + decode(rb.at[3], BELOW) + decode(rb.at[2], BELOW))
    code(below, qs, BELOW)

    @pl.when(chip < CHIPS - 1)
    def _():
        shift.start()

    a_all.wait_recv()
    total[...] = merged[0, :OWN, :] + (decode(ra.at[1], OWN) + decode(ra.at[3], OWN) + decode(ra.at[2], OWN))

    z_all = remote(pz.at[pl.ds(0, NZ - 1)], pz.at[pl.ds(0, NZ - 1)], z_s.at[0], z_r.at[0], sib)
    z_all.wait_recv()
    part = ((pz[0] + pz[1]) + (pz[2] + pz[3])) + ((pz[4] + pz[5]) + (pz[6] + pz[7]))
    pout[core, mine, :] = part * F32(1.0 / math.sqrt(LIVE))
    xy_back = [
        remote(pout.at[core, mine], pout.at[core, mine], xy_s.at[1], xy_r.at[1], at(dx, dy))
        for i, (dx, dy) in enumerate(xys)
    ]
    for copy in xy_back:
        copy.start()

    @pl.when(chip > 0)
    def _():
        shift.wait_recv()
        total[:BELOW, :] += decode(rs, BELOW)

    slot = NX * core + p
    code(total[pl.ds(BR * (1 - core), BR), :], other, BR)
    code(total[pl.ds(BR * core, BR), :], all_q.at[slot], BR)
    gather = []
    for dx in order:
        gather.append(remote(other, all_q.at[slot], ag_s.at[0], ag_r.at[0], at(dx, band=sb)))
        if dx:
            gather.append(remote(all_q.at[slot], all_q.at[slot], ag_s.at[0], ag_r.at[0], at(dx)))
    for copy in gather:
        copy.start()

    for copy in (z_all, a_all, b_all):
        copy.wait_send()

    @pl.when(chip < CHIPS - 1)
    def _():
        shift.wait_send()

    back_all = remote(pxy, pxy, xy_s.at[1], xy_r.at[1], sib)
    back_all.wait_recv()
    last = remote(pout.at[core], pout.at[core], pc_s.at[1], pc_r.at[1], sib)
    last.start()
    gather_all = remote(all_q.at[pl.ds(0, 2 * NX - 1)], all_q.at[pl.ds(0, 2 * NX - 1)], ag_s.at[0], ag_r.at[0], sib)
    gather_all.wait_recv()
    for copy in (gather_all, back_all):
        copy.wait_send()
    last.wait()


def finish_kernel(all_q, psum, out, pout, buf, sems):
    probe_copy = pltpu.make_async_copy(psum, pout, sems.at[2])
    probe_copy.start()
    copies = []
    for plane in range(2):
        for c in range(2):
            for j in range(2):
                block = 2 * c + j
                cols = slice(block * LANES, (block + 1) * LANES)
                buf[plane, :, cols] = decode(all_q.at[NX * c + 2 * plane + j], BR)
        copies.append(pltpu.make_async_copy(buf.at[plane], out.at[plane], sems.at[plane]))
        copies[plane].start()
    for copy in copies + [probe_copy]:
        copy.wait()


VM = pl.BlockSpec(memory_space=pltpu.VMEM)
SM = pl.BlockSpec(memory_space=pltpu.SMEM)
HBM = pl.BlockSpec(memory_space=pltpu.HBM)
DMA = pltpu.SemaphoreType.DMA


def params(cid=None):
    return pltpu.CompilerParams(vmem_limit_bytes=40 << 20, collective_id=cid, has_side_effects=cid is not None)


def halo(obj, waves, probe, measured, rows, cols):
    return pl.pallas_call(
        halo_kernel,
        out_shape=(
            jax.ShapeDtypeStruct((2, BLOCKS, ROWS, LANES), F32),
            jax.ShapeDtypeStruct((2 * W, 2 * W), BF16),
            jax.ShapeDtypeStruct((2 * W, 2 * W), BF16),
            jax.ShapeDtypeStruct(probe.shape, probe.dtype),
            jax.ShapeDtypeStruct(measured.shape, measured.dtype),
            jax.ShapeDtypeStruct(rows.shape, rows.dtype),
            jax.ShapeDtypeStruct(cols.shape, cols.dtype),
        ),
        in_specs=[HBM] * 6,
        out_specs=(VM, VM, VM, VM, VM, SM, SM),
        scratch_shapes=[
            pltpu.VMEM((2, BR, NCOLS), F32),
            pltpu.VMEM((W, 2 * W), F32),
            pltpu.VMEM((2, BR, NCOLS), BF16),
            pltpu.VMEM((2, BR, NCOLS), BF16),
            pltpu.VMEM((2, TAIL, NCOLS), BF16),
            DMA((4,)),
            DMA((3,)),
            DMA((7,)),
        ],
        compiler_params=params(0),
        name="halo",
    )(obj, waves, probe, measured, rows, cols)


def slots(counts, rows, cols, win, probe, measured, left, right):
    return pl.pallas_call(
        slots_kernel,
        out_shape=(
            jax.ShapeDtypeStruct((2, BLOCKS, ROWS, LANES), F32),
            jax.ShapeDtypeStruct((2, W, W), F32),
        ),
        in_specs=[SM, SM, SM, VM, VM, VM, VM, VM],
        out_specs=(VM, VM),
        compiler_params=params(),
        name="slots",
    )(counts, rows, cols, win, probe, measured, left, right)


def merge(counts, rows, cols, win, probe, measured, left, right, grad, psum):
    coded = lambda n, *lead: pltpu.VMEM((*lead, n + EXTRA, LANES), jnp.int16)
    piece = lambda n, *lead: pltpu.VMEM((*lead, n, LANES), F32)
    flat = lambda n, *lead: pltpu.VMEM((*lead, n, W), F32)
    return pl.pallas_call(
        merge_kernel,
        out_shape=(
            jax.ShapeDtypeStruct((2 * NX, BR + EXTRA, LANES), jnp.int16),
            jax.ShapeDtypeStruct((2, W, W), F32),
        ),
        in_specs=[SM] * 3 + [VM] * 7,
        out_specs=(VM, VM),
        scratch_shapes=[
            piece(W + 2 * BR, GROUP, 2, BLOCKS), flat(W, 2),
            piece(ROWS, NX), piece(ROWS, NX), piece(CHIP, NX),
            coded(OWN, NX), coded(BELOW, NX), coded(OWN, NX), coded(BELOW, NX), coded(BELOW), coded(BELOW),
            piece(OWN), coded(BR),
            flat(W), flat(W), flat(16, 15), flat(16, NZ),
        ]
        + [DMA((NX,))] * 2
        + [DMA((1,))] * 8
        + [DMA((2,))] * 4
        + [DMA((1,))] * 2,
        compiler_params=params(1),
        name="merge",
    )(counts, rows, cols, win, probe, measured, left, right, grad, psum)


def finish(all_q, psum):
    return pl.pallas_call(
        finish_kernel,
        out_shape=(
            jax.ShapeDtypeStruct((2, BR, NCOLS), F32),
            jax.ShapeDtypeStruct((2, W, W), F32),
        ),
        in_specs=[VM, VM],
        out_specs=(HBM, HBM),
        scratch_shapes=[pltpu.VMEM((2, BR, NCOLS), F32), DMA((3,))],
        compiler_params=params(),
        name="finish",
    )(all_q, psum)


def on_device(object_field, probe, measured, row_offset, col_offset, counts):
    win, left, right, probe, measured, rows, cols = halo(
        *[
            pltpu.with_memory_space_constraint(v, pltpu.HBM)
            for v in (object_field, jnp.asarray(table()), probe, measured, row_offset, col_offset)
        ]
    )
    grad, psum = slots(counts, rows, cols, win, probe, measured, left, right)
    return finish(*merge(counts, rows, cols, win, probe, measured, left, right, grad, psum))


def solution(mesh):
    placed = (
        P(None, "band", None),
        P(),
        P(("band", "pos"), None, None),
        P(("band", "pos")),
        P(("band", "pos")),
        P(("band", "pos")),
    )
    return jax.shard_map(
        on_device,
        mesh=mesh,
        in_specs=placed,
        out_specs=(P(None, "band", None), P()),
        check_vma=False,
    )
```

```python
import math

import jax
import jax.numpy as jnp
import ml_dtypes
import numpy as np
from jax import lax
from jax.experimental import pallas as pl
from jax.experimental.pallas import tpu as pltpu
from jax.sharding import PartitionSpec as P

W = 256
BR = 192
NCOLS = 512
CAP = 12
GROUP = 6
LIVE = 1024
LANES = 128
BLOCKS = NCOLS // LANES
TAIL = 64
ROWS = 2 * BR + TAIL
OWN = 2 * BR
BELOW = BR + TAIL
CHIP = OWN + BELOW
EXTRA = 16
TINY = 1e-33
FULL = 16000.0
NX, NY, NZ = 4, 4, 8
CHIPS = NY * NZ
BANDS = 2 * CHIPS
F32 = jnp.float32
BF16 = jnp.bfloat16
MESH = pl.DeviceIdType.MESH


def table():
    index = np.arange(W, dtype=np.int32)
    phase = index[:, None] * index[None, :] % W
    angle = phase.astype(np.float32) * np.float32(2.0 * math.pi / W)
    factor = np.float32(1.0 / math.sqrt(W))
    real = (np.cos(angle) * factor).astype(ml_dtypes.bfloat16)
    imag = (-np.sin(angle) * factor).astype(ml_dtypes.bfloat16)
    return np.concatenate([real, imag], 1).astype(np.float32)


def dot(a, b):
    return jnp.dot(a, b, preferred_element_type=F32)


def remote(src, dst, send, recv, device):
    return pltpu.make_async_remote_copy(
        src_ref=src, dst_ref=dst, send_sem=send, recv_sem=recv, device_id=device, device_id_type=MESH
    )


def signal(barrier, device):
    pl.semaphore_signal(barrier, inc=1, device_id=device, device_id_type=MESH)


def halo_kernel(
    obj, table, probe_in, meas_in, row_in, col_in,
    win, left, right, probe, meas, row, col,
    own, waves, low, near, far, send, recv, load,
):
    b = lax.axis_index("band")
    odd = lax.rem(b, 2)
    barrier = pltpu.get_barrier_semaphore()

    @pl.when(b + 1 < BANDS)
    def _():
        signal(barrier, {"band": b + 1})

    @pl.when((odd == 1) & (b + 2 < BANDS))
    def _():
        signal(barrier, {"band": b + 2})

    loads = [pltpu.make_async_copy(obj.at[plane], own.at[plane], load.at[plane]) for plane in range(2)]
    rest = ((table, waves), (row_in, row), (col_in, col), (probe_in, probe), (meas_in, meas))
    loads += [pltpu.make_async_copy(src, dst, load.at[2 + i]) for i, (src, dst) in enumerate(rest)]
    for copy in loads:
        copy.start()
    for plane in range(2):
        loads[plane].wait()
        low[plane] = own[plane].astype(BF16)

    head, rest_rows = pl.ds(0, TAIL), pl.ds(TAIL, BR - TAIL)
    above = [
        remote(low.at[:, rows], near.at[:, rows], send.at[i], recv.at[i], {"band": b - 1})
        for i, rows in enumerate((head, rest_rows))
    ]
    skip = remote(low.at[:, head], far, send.at[2], recv.at[2], {"band": b - 2})
    relay = remote(near.at[:, head], far, send.at[3], recv.at[2], {"band": b - 1})

    @pl.when(b > 0)
    def _():
        pl.semaphore_wait(barrier, jnp.where((odd == 1) & (b > 2), 2, 1))

    @pl.when((odd == 1) & (b > 2))
    def _():
        skip.start()

    @pl.when(b > 0)
    def _():
        for copy in above:
            copy.start()

    loads[2].wait()
    real, imag = waves[:, :W], waves[:, W:]
    for rows, first, second in ((0, real, imag), (W, -imag, real)):
        right[rows : rows + W, :W] = first.astype(BF16)
        right[rows : rows + W, W:] = second.astype(BF16)
    for rows, first, second in ((0, real, -imag), (W, imag, real)):
        left[rows : rows + W, :W] = first.astype(BF16)
        left[rows : rows + W, W:] = second.astype(BF16)

    def fill(src, top, count):
        for plane in range(2):
            for block in range(BLOCKS):
                win[plane, block, top : top + count] = src[plane, :, block * LANES : (block + 1) * LANES].astype(F32)

    fill(low, 0, BR)

    @pl.when(b + 1 < BANDS)
    def _():
        above[0].wait_recv()

        @pl.when(odd == 1)
        def _():
            relay.start()

        fill(near.at[:, head], BR, TAIL)
        above[1].wait_recv()
        fill(near.at[:, rest_rows], BR + TAIL, BR - TAIL)

    @pl.when(b + 1 >= BANDS)
    def _():
        win[:, :, BR : 2 * BR] = jnp.zeros((2, BLOCKS, BR, LANES), F32)

    @pl.when(b + 2 < BANDS)
    def _():
        skip.wait_recv()
        fill(far, 2 * BR, TAIL)

    @pl.when(b + 2 >= BANDS)
    def _():
        win[:, :, 2 * BR :] = jnp.zeros((2, BLOCKS, TAIL, LANES), F32)

    for copy in loads[3:]:
        copy.wait()

    @pl.when(b > 0)
    def _():
        for copy in above:
            copy.wait_send()

    @pl.when((odd == 1) & (b > 2))
    def _():
        skip.wait_send()

    @pl.when((odd == 1) & (b + 1 < BANDS))
    def _():
        relay.wait_send()


def run_group(base, n, row, col, win, probe, meas, left, right, psum, put):
    lane = lax.broadcasted_iota(jnp.int32, (W, LANES), 1)
    place, patches, half, resid, spread, chi = ({} for _ in range(6))

    def enter(k):
        s = base + k
        c = col[s]
        block = jnp.where(c >= LANES, 1, 0)
        place[k] = (row[s], block, c - LANES * block)
        r, block, shift = place[k]
        back = lax.rem(LANES - shift, LANES)
        head = lane < LANES - shift
        patch = []
        for plane in range(2):
            parts = [pltpu.roll(win[plane, block + j, pl.ds(r, W), :], back, 1) for j in range(3)]
            patch.append(
                jnp.concatenate([jnp.where(head, parts[0], parts[1]), jnp.where(head, parts[1], parts[2])], 1)
            )
        patches[k] = patch
        pr, pi = patch
        qr, qi = probe[0], probe[1]
        exit_wave = jnp.concatenate([qr * pr - qi * pi, qr * pi + qi * pr], 0).astype(BF16)
        half[k] = dot(left[...], exit_wave).astype(BF16)

    def detect(k):
        wave = dot(jnp.concatenate([half[k][:W], half[k][W:]], 1), right[...])
        wr, wi = wave[:, :W], wave[:, W:]
        live = jnp.where(base + k < n, F32(1.0), F32(0.0))
        excess = (wr * wr + wi * wi - meas[base + k].astype(F32)) * live
        resid[k] = jnp.concatenate([wr * excess, wi * excess], 1).astype(BF16)

    def over_columns(k):
        spread[k] = dot(resid[k], left[...]).astype(BF16)

    def over_rows(k):
        chi[k] = dot(right[...], jnp.concatenate([spread[k][:, :W], spread[k][:, W:]], 0))

    def leave(k):
        r, block, shift = place[k]
        ahead = lax.rem(shift, LANES)
        tail = lane >= shift
        pr, pi = patches[k]
        qr, qi = probe[0], probe[1]
        cr, ci = chi[k][:W], chi[k][W:]
        psum[0] += pr * cr + pi * ci
        psum[1] += pr * ci - pi * cr
        for plane, g in enumerate((qr * cr + qi * ci, qr * ci - qi * cr)):
            g0 = pltpu.roll(g[:, :LANES], ahead, 1)
            g1 = pltpu.roll(g[:, LANES:], ahead, 1)
            parts = jnp.where(tail, g0, 0.0), jnp.where(tail, g1, g0), jnp.where(tail, 0.0, g1)
            put(k, plane, r, block, parts)

    stages = (enter, detect, over_columns, over_rows, leave)
    for t in range(GROUP + len(stages) - 1):
        for at in reversed(range(len(stages))):
            if 0 <= t - at < GROUP:
                stages[at](t - at)


def slots_kernel(cnt, row, col, win, probe, meas, left, right, grad, psum):
    grad[...] = jnp.zeros_like(grad)
    psum[...] = jnp.zeros_like(psum)
    n = cnt[0]

    def put(k, plane, r, block, parts):
        for j, part in enumerate(parts):
            grad[plane, block + j, pl.ds(r, W), :] += part

    def group(i, carry):
        run_group(GROUP * (i + 1), n, row, col, win, probe, meas, left, right, psum, put)
        return carry

    lax.fori_loop(0, (n - 1) // GROUP, group, 0)


def signed_power(value):
    most = jnp.maximum(jnp.max(jnp.abs(value), axis=0, keepdims=True), F32(TINY))
    return jnp.floor(jnp.log2(most))


def code(value, dst, rows):
    power = signed_power(value)
    scaled = value * (jnp.exp2(-power) * F32(FULL))
    dst[:rows] = jnp.round(scaled).astype(jnp.int32).astype(jnp.int16)
    dst[rows:] = jnp.broadcast_to(power, (EXTRA, LANES)).astype(jnp.int32).astype(jnp.int16)


def decode(src, rows, first=0, last=None):
    last = rows if last is None else last
    power = src[rows:].astype(jnp.int32).astype(F32)[:1]
    return src[first:last].astype(jnp.int32).astype(F32) * (jnp.exp2(power) * F32(1.0 / FULL))


def merge_kernel(
    cnt, row, col, win, probe, meas, left, right, grad, psum_in, full_q, early_q, late_q, pout,
    spots, psum, to_core_buf, from_core, merged, qa, qb, ra, rb, qs, rs, total, full, early, late,
    pcore, psumc, pxy, pz,
    core_s, core_r, a_s, a_r, b_s, b_r, sh_s, sh_r, ag_s, ag_r, pc_s, pc_r, xy_s, xy_r, z_s, z_r,
):
    b = lax.axis_index("band")
    p = lax.axis_index("pos")
    core = lax.rem(b, 2)
    chip = b // 2
    z = lax.rem(chip, NZ)
    y = chip // NZ
    sb = b + 1 - 2 * core
    sib = {"band": sb}

    def at(dx, dy=0, **more):
        device = dict(more)
        if dx:
            device["pos"] = lax.rem(p + dx, NX)
        if dy:
            device["band"] = b + 2 * NZ * (lax.rem(y + dy, NY) - y)
        return device

    hops = (0, 1, 2, 1)
    xys = [(dx, dy) for dy in range(NY) for dx in range(NX) if dx or dy]
    xys.sort(key=lambda d: -hops[d[0]] - hops[d[1]])
    zdev = [None] + [{"band": b + 2 * (lax.rem(z + d, NZ) - z)} for d in range(1, NZ)]

    barrier = pltpu.get_barrier_semaphore()
    for device in [at(dx, band=sb) for dx in range(NX)] + [at(*d) for d in xys] + zdev[1:]:
        signal(barrier, device)
    @pl.when(chip > 0)
    def _():
        signal(barrier, {"band": b - 2})

    for k in range(GROUP):
        spots[k, :, :, :BR, :] = jnp.zeros((2, BLOCKS, BR, LANES), F32)
        spots[k, :, :, BR + W :, :] = jnp.zeros((2, BLOCKS, BR, LANES), F32)
    psum[...] = psum_in[...]
    middle = pl.ds(BR, W)

    def put(k, plane, r, block, parts):
        second = block > 0
        a, c, d = parts
        zero = jnp.zeros_like(a)
        for j, (low, high) in enumerate(((a, zero), (c, a), (d, c), (zero, d))):
            spots[k, plane, j, middle, :] = jnp.where(second, high, low)

    run_group(0, cnt[0], row, col, win, probe, meas, left, right, psum, put)

    def window(plane, block):
        total = grad[plane, block]
        for k in range(GROUP):
            total = total + spots[k, plane, block, pl.ds(BR - row[k], ROWS), :]
        return total

    pl.semaphore_wait(barrier, NX + NX * NY - 1 + NZ - 1 + jnp.minimum(CHIPS - 1 - chip, 1))

    quarters = (2, 1, 3, 0)

    def quarter(dy):
        return pl.ds(W // NY * lax.rem(y + dy + NY, NY), W // NY)

    first = [
        remote(psum.at[1 - core, quarter(dy)], pcore.at[quarter(dy)], pc_s.at[dy], pc_r.at[dy], sib) for dy in range(NY)
    ]
    for dy in quarters:
        first[dy].start()
    piece = [lax.rem(p + dx, NX) for dx in range(NX)]
    order = (2, 1, 3, 0)
    to_core = {
        dx: remote(to_core_buf.at[dx], from_core.at[dx], core_s.at[dx], core_r.at[dx], sib) for dx in order
    }
    xy_send = {}
    for dy in quarters:
        first[dy].wait_recv()
        psumc[quarter(dy), :] = psum[core, quarter(dy), :] + pcore[quarter(dy), :]
        for i, d in enumerate(xys):
            if d[1] == dy:
                rows = pl.ds(16 * (NX * lax.rem(y + dy, NY) + lax.rem(p + d[0], NX)), 16)
                xy_send[d] = remote(psumc.at[rows], pxy.at[i], xy_s.at[NY], xy_r.at[NY], at(*d))
                xy_send[d].start()

    for dx in order:
        to_core_buf[dx] = window(piece[dx] // 2, 2 * (1 - core) + lax.rem(piece[dx], 2))
        to_core[dx].start()

    a_send = {dx: remote(qa.at[dx], ra.at[dx], a_s.at[0], a_r.at[0], at(dx)) for dx in (2, 1, 3)}
    b_send = {dx: remote(qb.at[dx], rb.at[dx], b_s.at[0], b_r.at[0], at(dx)) for dx in (2, 1, 3)}
    shift = remote(qs, rs, sh_s.at[0], sh_r.at[0], {"band": b + 2})
    for dx in order:
        merged[dx, pl.ds(ROWS * (1 - core), BR), :] = jnp.zeros((BR, LANES), F32)
        merged[dx, pl.ds(BR * core, ROWS), :] = window(piece[dx] // 2, 2 * core + lax.rem(piece[dx], 2))
        to_core[dx].wait_recv()
        merged[dx, pl.ds(BR * (1 - core), ROWS), :] += from_core[dx]
        if dx:
            code(merged[dx, OWN:, :], qb.at[dx], BELOW)
            b_send[dx].start()
    for dx in order[:3]:
        code(merged[dx, :OWN, :], qa.at[dx], OWN)
        a_send[dx].start()

    mine = pl.ds(16 * (NX * y + p), 16)
    xy_all = remote(pxy, pxy, xy_s.at[NY], xy_r.at[NY], sib)
    xy_all.wait_recv()
    part = psumc[mine, :]
    for i in range(len(xys)):
        part = part + pxy[i]
    pz[z] = part
    z_send = [remote(pz.at[z], pz.at[z], z_s.at[0], z_r.at[0], zdev[d]) for d in (4, 3, 5, 2, 6, 1, 7)]
    for copy in z_send:
        copy.start()

    for copy in first + [xy_all] + list(to_core.values()):
        copy.wait_send()
    others = pl.ds(1, NX - 1)
    a_all = remote(ra.at[others], ra.at[others], a_s.at[0], a_r.at[0], sib)
    b_all = remote(rb.at[others], rb.at[others], b_s.at[0], b_r.at[0], sib)
    b_all.wait_recv()
    below = merged[0, OWN:, :] + (decode(rb.at[1], BELOW) + decode(rb.at[3], BELOW) + decode(rb.at[2], BELOW))
    code(below, qs, BELOW)

    @pl.when(chip < CHIPS - 1)
    def _():
        shift.start()

    a_all.wait_recv()
    total[...] = merged[0, :OWN, :] + (decode(ra.at[1], OWN) + decode(ra.at[3], OWN) + decode(ra.at[2], OWN))

    slot = NX * core + p
    even_band, odd_band = {"band": 2 * chip}, {"band": 2 * chip + 1}

    def spread(src, dst, lead, k, here):
        copies = [remote(src, dst.at[slot], ag_s.at[k], ag_r.at[k], at(dx, **lead)) for dx in order]
        for copy in copies[:-1]:
            copy.start()

        @pl.when(core != here)
        def _():
            copies[-1].start()

        @pl.when(core == here)
        def _():
            dst[slot] = src[...]

    def settle(src, dst, k, here):
        @pl.when(core == here)
        def _():
            seven = dst.at[pl.ds(0, 2 * NX - 1)]
            remote(seven, seven, ag_s.at[k], ag_r.at[k], sib).wait_recv()

        for count, mine_ in ((NX, 1 - here), (NX - 1, here)):

            @pl.when(core == mine_)
            def _():
                some = dst.at[pl.ds(0, count)]
                remote(some, some, ag_s.at[k], ag_r.at[k], sib).wait_send()

    code(total[BELOW:, :], early, OWN - BELOW)
    spread(early, early_q, odd_band, 0, 1)

    z_all = remote(pz.at[pl.ds(0, NZ - 1)], pz.at[pl.ds(0, NZ - 1)], z_s.at[0], z_r.at[0], sib)
    z_all.wait_recv()
    part = ((pz[0] + pz[1]) + (pz[2] + pz[3])) + ((pz[4] + pz[5]) + (pz[6] + pz[7]))
    pout[core, mine, :] = part * F32(1.0 / math.sqrt(LIVE))
    xy_back = [
        remote(pout.at[core, mine], pout.at[core, mine], xy_s.at[dy], xy_r.at[dy], at(dx, dy))
        for i, (dx, dy) in enumerate(xys)
    ]
    for copy in xy_back:
        copy.start()

    @pl.when(chip > 0)
    def _():
        shift.wait_recv()
        total[:BELOW, :] += decode(rs, BELOW)

    code(total[:BR, :], full, BR)
    spread(full, full_q, even_band, 1, 0)
    code(total[BR:BELOW, :], late, TAIL)
    spread(late, late_q, odd_band, 2, 1)

    for copy in (z_all, a_all, b_all):
        copy.wait_send()

    @pl.when(chip < CHIPS - 1)
    def _():
        shift.wait_send()

    back = []
    last = []
    for dy in (0, 1, 3, 2):
        some = pxy.at[pl.ds(0, NX if dy else NX - 1)]
        back.append(remote(some, some, xy_s.at[dy], xy_r.at[dy], sib))
        back[-1].wait_recv()
        rows = quarter(-dy)
        last.append(remote(pout.at[core, rows], pout.at[core, rows], pc_s.at[NY + dy], pc_r.at[NY + dy], sib))
        last[-1].start()
    settle(early, early_q, 0, 1)
    settle(full, full_q, 1, 0)
    settle(late, late_q, 2, 1)
    for copy in back:
        copy.wait_send()
    for copy in last:
        copy.wait()


def finish_kernel(full_q, early_q, late_q, psum, out, pout, buf, sems):
    core = lax.rem(lax.axis_index("band"), 2)
    probe_copy = pltpu.make_async_copy(psum, pout, sems.at[2])
    probe_copy.start()
    copies = []
    for plane in range(2):
        for c in range(2):
            for j in range(2):
                block = 2 * c + j
                cols = slice(block * LANES, (block + 1) * LANES)
                k = NX * c + 2 * plane + j

                @pl.when(core == 0)
                def _():
                    buf[plane, :, cols] = decode(full_q.at[k], BR)

                @pl.when(core == 1)
                def _():
                    buf[plane, :TAIL, cols] = decode(late_q.at[k], TAIL)
                    buf[plane, TAIL:, cols] = decode(early_q.at[k], BR - TAIL)

        copies.append(pltpu.make_async_copy(buf.at[plane], out.at[plane], sems.at[plane]))
        copies[plane].start()
    for copy in copies + [probe_copy]:
        copy.wait()


VM = pl.BlockSpec(memory_space=pltpu.VMEM)
SM = pl.BlockSpec(memory_space=pltpu.SMEM)
HBM = pl.BlockSpec(memory_space=pltpu.HBM)
DMA = pltpu.SemaphoreType.DMA


def params(cid=None):
    return pltpu.CompilerParams(vmem_limit_bytes=40 << 20, collective_id=cid, has_side_effects=cid is not None)


def halo(obj, waves, probe, measured, rows, cols):
    return pl.pallas_call(
        halo_kernel,
        out_shape=(
            jax.ShapeDtypeStruct((2, BLOCKS, ROWS, LANES), F32),
            jax.ShapeDtypeStruct((2 * W, 2 * W), BF16),
            jax.ShapeDtypeStruct((2 * W, 2 * W), BF16),
            jax.ShapeDtypeStruct(probe.shape, probe.dtype),
            jax.ShapeDtypeStruct(measured.shape, measured.dtype),
            jax.ShapeDtypeStruct(rows.shape, rows.dtype),
            jax.ShapeDtypeStruct(cols.shape, cols.dtype),
        ),
        in_specs=[HBM] * 6,
        out_specs=(VM, VM, VM, VM, VM, SM, SM),
        scratch_shapes=[
            pltpu.VMEM((2, BR, NCOLS), F32),
            pltpu.VMEM((W, 2 * W), F32),
            pltpu.VMEM((2, BR, NCOLS), BF16),
            pltpu.VMEM((2, BR, NCOLS), BF16),
            pltpu.VMEM((2, TAIL, NCOLS), BF16),
            DMA((4,)),
            DMA((3,)),
            DMA((7,)),
        ],
        compiler_params=params(0),
        name="halo",
    )(obj, waves, probe, measured, rows, cols)


def slots(counts, rows, cols, win, probe, measured, left, right):
    return pl.pallas_call(
        slots_kernel,
        out_shape=(
            jax.ShapeDtypeStruct((2, BLOCKS, ROWS, LANES), F32),
            jax.ShapeDtypeStruct((2, W, W), F32),
        ),
        in_specs=[SM, SM, SM, VM, VM, VM, VM, VM],
        out_specs=(VM, VM),
        compiler_params=params(),
        name="slots",
    )(counts, rows, cols, win, probe, measured, left, right)


def merge(counts, rows, cols, win, probe, measured, left, right, grad, psum):
    coded = lambda n, *lead: pltpu.VMEM((*lead, n + EXTRA, LANES), jnp.int16)
    piece = lambda n, *lead: pltpu.VMEM((*lead, n, LANES), F32)
    flat = lambda n, *lead: pltpu.VMEM((*lead, n, W), F32)
    return pl.pallas_call(
        merge_kernel,
        out_shape=(
            jax.ShapeDtypeStruct((2 * NX, BR + EXTRA, LANES), jnp.int16),
            jax.ShapeDtypeStruct((2 * NX, BR - TAIL + EXTRA, LANES), jnp.int16),
            jax.ShapeDtypeStruct((2 * NX, TAIL + EXTRA, LANES), jnp.int16),
            jax.ShapeDtypeStruct((2, W, W), F32),
        ),
        in_specs=[SM] * 3 + [VM] * 7,
        out_specs=(VM, VM, VM, VM),
        scratch_shapes=[
            piece(W + 2 * BR, GROUP, 2, BLOCKS), flat(W, 2),
            piece(ROWS, NX), piece(ROWS, NX), piece(CHIP, NX),
            coded(OWN, NX), coded(BELOW, NX), coded(OWN, NX), coded(BELOW, NX), coded(BELOW), coded(BELOW),
            piece(OWN), coded(BR), coded(BR - TAIL), coded(TAIL),
            flat(W), flat(W), flat(16, 15), flat(16, NZ),
        ]
        + [DMA((NX,))] * 2
        + [DMA((1,))] * 6
        + [DMA((3,))] * 2
        + [DMA((2 * NY,))] * 2
        + [DMA((NY + 1,))] * 2
        + [DMA((1,))] * 2,
        compiler_params=params(1),
        name="merge",
    )(counts, rows, cols, win, probe, measured, left, right, grad, psum)


def finish(full_q, early_q, late_q, psum):
    return pl.pallas_call(
        finish_kernel,
        out_shape=(
            jax.ShapeDtypeStruct((2, BR, NCOLS), F32),
            jax.ShapeDtypeStruct((2, W, W), F32),
        ),
        in_specs=[VM] * 4,
        out_specs=(HBM, HBM),
        scratch_shapes=[pltpu.VMEM((2, BR, NCOLS), F32), DMA((3,))],
        compiler_params=params(),
        name="finish",
    )(full_q, early_q, late_q, psum)


def on_device(object_field, probe, measured, row_offset, col_offset, counts):
    win, left, right, probe, measured, rows, cols = halo(
        *[
            pltpu.with_memory_space_constraint(v, pltpu.HBM)
            for v in (object_field, jnp.asarray(table()), probe, measured, row_offset, col_offset)
        ]
    )
    grad, psum = slots(counts, rows, cols, win, probe, measured, left, right)
    return finish(*merge(counts, rows, cols, win, probe, measured, left, right, grad, psum))


def solution(mesh):
    placed = (
        P(None, "band", None),
        P(),
        P(("band", "pos"), None, None),
        P(("band", "pos")),
        P(("band", "pos")),
        P(("band", "pos")),
    )
    return jax.shard_map(
        on_device,
        mesh=mesh,
        in_specs=placed,
        out_specs=(P(None, "band", None), P()),
        check_vma=False,
    )
```
